32 devices in a mesh: groups: 2 (over y), imp: 4 (over z), camp: 2 (over x), rep: 2 (over core).
Axes of the slice: x: 2, y: 2, z: 4, core: 2. Of those that a mesh axis runs over, the one named last changes fastest.
Arguments:
- imp_embed: bfloat16 [16384, 128], P(('groups', 'imp')), parts along dimension 0, may hold values from -7 to 7
- camp_embed: bfloat16 [32, 1024, 128], P(('groups', 'camp'), 'imp'), parts along dimension 0, may hold values from -5 to 5
- capacity: int32 [32768], P(('groups', 'camp')), parts along dimension 0, may hold values from 1 to 8
- tile_lists: int32 [8, 2, 2, 2, 2], P(('groups', 'imp'), 'camp', 'rep'), parts along dimension 0, may hold values from 0 to 7, as said below
- tile_counts: int32 [8, 2, 2, 2], P(('groups', 'imp'), 'camp', 'rep'), parts along dimension 0, may hold values from 1 to 2, as said below
Outputs:
- row_potential: float32 [16384], P(('groups', 'imp')), parts along dimension 0
- column_potential: float32 [32768], P(('groups', 'camp')), parts along dimension 0
The draws below stay inside these ranges and needn't reach their ends.
There are 2 independent parts, one for each index of `groups`. The reference program is written for one: setup_inputs(seed, part) draws one part's arguments, and reference() takes and returns one part's arrays. A program takes and returns all parts, laid end to end along the dimension named above; each array names one. Nothing has to cross between parts.
Inputs may be any that keep to these rules, and one draw needn't show every extreme that they name: `tile_lists`: entries are campaign tiles inside the campaign block. For one impression block, campaign block and impression tile, the 4 entries of both list halves are all different. Entries past the count are not eligible. `tile_counts`: some list reaches 2 in every draw.
All inputs are finite; a program needn't handle non-finite values.
Results may differ from the reference program's by a relative error of at most 0.0003.
Values may be sent and summed in bfloat16 or wider, within the bound.
A program may use at most 64 MiB of HBM per device.

```python
import jax
import jax.numpy as jnp
from jax import lax

E = 128
TILE = 1024
RT_DEV = 2
CT_DEV = 8
SLOTS = 2
ITERS = 2
CAMPAIGNS = 16384
N_IMP = 4
N_CAMP = 2
N_REP = 2


def draw_imp_embed(key, part):
    key = jax.random.fold_in(key, 5)
    values = jnp.clip(jax.random.normal(key, (N_IMP * RT_DEV * TILE, E), jnp.float32), -6.0, 6.0)
    return values.astype(jnp.bfloat16)


def draw_camp_embed(key, part):
    key = jax.random.fold_in(key, 7)
    factor = float(E) ** (-0.5)
    values = jnp.clip(jax.random.normal(key, (N_CAMP * CT_DEV, TILE, E), jnp.float32), -6.0, 6.0) * factor
    return jnp.clip(values, -5.0, 5.0).astype(jnp.bfloat16)


def draw_tile_lists(key, part):
    key = jax.random.fold_in(key, 11)
    tile_keys = jax.random.split(key, N_IMP * N_CAMP * RT_DEV)
    full_orders = jax.vmap(lambda subkey: jax.random.permutation(subkey, CT_DEV)[:2 * SLOTS])(tile_keys)
    short_orders = jax.vmap(lambda subkey: jax.random.permutation(jax.random.fold_in(subkey, 1), CT_DEV - 1)[:2 * SLOTS])(tile_keys)
    full_orders = full_orders.reshape(N_IMP, N_CAMP, RT_DEV, 2 * SLOTS)
    short_orders = short_orders.reshape(N_IMP, N_CAMP, RT_DEV, 2 * SLOTS)
    excluded = jax.random.randint(jax.random.fold_in(key, 2), (N_CAMP,), 0, CT_DEV)
    offset = jax.random.randint(jax.random.fold_in(key, 3), (), 0, 2)
    block_index = jnp.arange(N_CAMP, dtype=jnp.int32)
    thinned = (block_index + offset) % 2 == 0
    shifted = short_orders + (short_orders >= excluded[None, :, None, None]).astype(jnp.int32)
    orders = jnp.where(thinned[None, :, None, None], shifted, full_orders)
    first_half = orders[..., :SLOTS]
    second_half = orders[..., SLOTS:2 * SLOTS]
    return jnp.stack([first_half, second_half], axis=2).astype(jnp.int32)


def draw_tile_counts(key, part):
    key = jax.random.fold_in(key, 13)
    count_shape = (N_IMP, N_CAMP, N_REP, RT_DEV)
    heavier = jax.random.randint(key, count_shape, 0, 3) == 0
    imp_index = jax.lax.broadcasted_iota(jnp.int32, count_shape, 0)
    rep_index = jax.lax.broadcasted_iota(jnp.int32, count_shape, 2)
    forced = (imp_index % 4 == 0) & (rep_index == 0)
    return jnp.where(heavier | forced, SLOTS, 1).astype(jnp.int32)


def place_ends(drawn, stream_key, smallest, high):
    extent = drawn.shape
    place = [jax.random.randint(jax.random.fold_in(stream_key, axis), (), 0, extent[axis]) for axis in range(len(extent))]
    drawn = drawn.at[tuple(place)].set(smallest)
    longest = extent.index(max(extent))
    place[longest] = (place[longest] + 1) % extent[longest]
    return drawn.at[tuple(place)].set(high)


def setup_inputs(seed: int = 0, part: int = 0) -> dict:
    splits = jax.random.split(jax.random.key(seed), 6)
    part_keys = jax.random.split(jax.random.fold_in(splits[5], part), 6)
    return {
        "imp_embed": draw_imp_embed(jax.random.fold_in(jax.random.fold_in(splits[5], part), 71), part),
        "camp_embed": draw_camp_embed(jax.random.fold_in(jax.random.fold_in(splits[5], part), 71), part),
        "capacity": place_ends(jax.random.randint(part_keys[2], (CAMPAIGNS,), 1, 9), jax.random.fold_in(part_keys[2], 1), 1, 8).astype(jnp.int32),
        "tile_lists": draw_tile_lists(jax.random.fold_in(jax.random.fold_in(splits[5], part), 71), part),
        "tile_counts": draw_tile_counts(jax.random.fold_in(jax.random.fold_in(splits[5], part), 71), part),
    }


SMOOTHING = 0.5
CAP_UNIT = 0.25
LOWEST = -1e30


def reference(imp_embed, camp_embed, capacity, tile_lists, tile_counts):
    row_tiles = imp_embed.reshape(N_IMP * RT_DEV, TILE, E)
    list_shape = tile_lists.shape
    imp_index = lax.broadcasted_iota(jnp.int32, list_shape, 0)
    camp_index = lax.broadcasted_iota(jnp.int32, list_shape, 1)
    tile_row = lax.broadcasted_iota(jnp.int32, list_shape, 3)
    slot_index = lax.broadcasted_iota(jnp.int32, list_shape, 4)
    row_ids = (imp_index * RT_DEV + tile_row).reshape(-1).astype(jnp.int32)
    col_ids = (camp_index * CT_DEV + tile_lists).reshape(-1).astype(jnp.int32)
    live_slots = (slot_index < tile_counts[..., None]).reshape(-1)

    def row_sweep(col_pot):
        def one_slot(pair_ids):
            affinity = jnp.dot(row_tiles[pair_ids[0]], camp_embed[pair_ids[1]].T, preferred_element_type=jnp.float32)
            scores = (col_pot[pair_ids[1]][None, :] + affinity) / SMOOTHING
            highest = jnp.max(scores, axis=1)
            return highest, jnp.sum(jnp.exp(scores - highest[:, None]), axis=1)

        tile_highs, tile_sums = lax.map(one_slot, (row_ids, col_ids))
        tile_highs = jnp.where(live_slots[:, None], tile_highs, LOWEST)
        tile_sums = jnp.where(live_slots[:, None], tile_sums, 0.0)
        merged_high = jnp.full((N_IMP * RT_DEV, TILE), LOWEST, jnp.float32).at[row_ids].max(tile_highs)
        merged_sum = jnp.zeros((N_IMP * RT_DEV, TILE), jnp.float32).at[row_ids].add(tile_sums * jnp.exp(tile_highs - merged_high[row_ids]))
        return merged_high, merged_sum

    def column_sweep(row_pot):
        def one_slot(pair_ids):
            affinity = jnp.dot(row_tiles[pair_ids[0]], camp_embed[pair_ids[1]].T, preferred_element_type=jnp.float32)
            scores = (row_pot[pair_ids[0]][:, None] + affinity) / SMOOTHING
            highest = jnp.max(scores, axis=0)
            return highest, jnp.sum(jnp.exp(scores - highest[None, :]), axis=0)

        tile_highs, tile_sums = lax.map(one_slot, (row_ids, col_ids))
        tile_highs = jnp.where(live_slots[:, None], tile_highs, LOWEST)
        tile_sums = jnp.where(live_slots[:, None], tile_sums, 0.0)
        merged_high = jnp.full((N_CAMP * CT_DEV, TILE), LOWEST, jnp.float32).at[col_ids].max(tile_highs)
        merged_sum = jnp.zeros((N_CAMP * CT_DEV, TILE), jnp.float32).at[col_ids].add(tile_sums * jnp.exp(tile_highs - merged_high[col_ids]))
        return merged_high, merged_sum

    row_pot = jnp.zeros((N_IMP * RT_DEV, TILE), jnp.float32)
    col_pot = jnp.zeros((N_CAMP * CT_DEV, TILE), jnp.float32)
    log_cap = (SMOOTHING * jnp.log(CAP_UNIT * capacity.astype(jnp.float32))).reshape(N_CAMP * CT_DEV, TILE)
    for iteration in range(ITERS):
        merged_high, merged_sum = row_sweep(col_pot)
        row_pot = jnp.minimum(row_pot, -SMOOTHING * (merged_high + jnp.log(merged_sum)))
        merged_high, merged_sum = column_sweep(row_pot)
        has_rows = merged_sum > 0.0
        log_total = merged_high + jnp.log(jnp.where(has_rows, merged_sum, 1.0))
        col_pot = jnp.where(has_rows, jnp.minimum(col_pot, log_cap - SMOOTHING * log_total), col_pot)
    return row_pot.reshape(-1), col_pot.reshape(-1)
```

```python
import functools
import math

import jax
import jax.numpy as jnp
from jax import lax
from jax.experimental import pallas as pl
from jax.experimental.pallas import tpu as pltpu
from jax.sharding import PartitionSpec as P

ITERS = 2
LANES = 128
SCALE = 2.0 * math.log2(math.e)
UNSCALE = 1.0 / SCALE
LOWEST = -1e30
NO_ROWS = -1e29
MESH = pl.DeviceIdType.MESH


def lse_sublanes(x):
    high = jnp.max(x, axis=0, keepdims=True)
    return high + jnp.log2(jnp.sum(jnp.exp2(x - high), axis=0, keepdims=True))


def kernel(
    cfg,
    code_ref,
    imp_ref,
    camp_ref,
    cap_ref,
    row_out,
    col_out,
    imps,
    scores,
    picked,
    lse,
    parts,
    rows,
    col_shift,
    cap_shift,
    pair_shift,
    cols,
    z_send,
    z_recv,
    x_send,
    x_recv,
    c_send,
    c_recv,
    rs_send,
    rs_recv,
    ag_send,
    ag_recv,
    out_send,
    out_recv,
):
    n_imp, n_camp, n_rep, tiles, tile, rt_dev, slots = cfg
    kpd = tile // (n_imp * n_rep)
    nq = n_camp * n_rep
    n = n_imp * nq
    block = rt_dev * tile
    piece = block // nq
    rr = piece // LANES
    per_tile = n_rep * slots
    span = min(256, tile)
    z = lax.axis_index("imp")
    x = lax.axis_index("camp")
    c = lax.axis_index("rep")
    me = z * nq + x * n_rep + c

    def device(o):
        oz = lax.div(o, nq)
        rest = lax.rem(o, nq)
        return {"imp": oz, "camp": lax.div(rest, n_rep), "rep": lax.rem(rest, n_rep)}

    barrier = pltpu.get_barrier_semaphore()

    def greet(k, carry):
        o = lax.rem(me + k, n)
        pl.semaphore_signal(barrier, inc=1, device_id=device(o), device_id_type=MESH)
        return carry

    lax.fori_loop(1, n, greet, 0)
    pl.semaphore_wait(barrier, n - 1)

    def piece_rows(ox, oc):
        return pl.ds(pl.multiple_of((ox * n_rep + oc) * piece, piece), piece)

    def z_copy(k):
        other = lax.rem(z + k, n_imp)
        return pltpu.make_async_remote_copy(
            src_ref=imp_ref.at[piece_rows(x, c)],
            dst_ref=imps.at[z, piece_rows(x, c)],
            send_sem=z_send.at[k],
            recv_sem=z_recv.at[n_imp - k],
            device_id={"imp": other, "camp": x, "rep": c},
            device_id_type=MESH,
        )

    def x_copy(k, dx):
        src = lax.rem(z + k, n_imp)
        ref = imps.at[src, piece_rows(x, c)]
        return pltpu.make_async_remote_copy(
            src_ref=ref,
            dst_ref=ref,
            send_sem=x_send.at[k, dx],
            recv_sem=x_recv.at[k, n_camp - dx],
            device_id={"imp": z, "camp": lax.rem(x + dx, n_camp), "rep": c},
            device_id_type=MESH,
        )

    def c_copy(k, dx, dc):
        src = lax.rem(z + k, n_imp)
        ref = imps.at[src, piece_rows(lax.rem(x + dx, n_camp), c)]
        return pltpu.make_async_remote_copy(
            src_ref=ref,
            dst_ref=ref,
            send_sem=c_send.at[k, dx, dc],
            recv_sem=c_recv.at[k, dx, n_rep - dc],
            device_id={"imp": z, "camp": x, "rep": lax.rem(c + dc, n_rep)},
            device_id_type=MESH,
        )

    def wait_z(k):
        ref = imps.at[lax.rem(z + k, n_imp), piece_rows(x, c)]
        pltpu.make_async_copy(ref, ref, z_recv.at[k]).wait()

    def wait_x(k, dx):
        ref = imps.at[lax.rem(z + k, n_imp), piece_rows(lax.rem(x + dx, n_camp), c)]
        pltpu.make_async_copy(ref, ref, x_recv.at[k, dx]).wait()

    def wait_c(k, dx, dc):
        ref = imps.at[
            lax.rem(z + k, n_imp),
            piece_rows(lax.rem(x + dx, n_camp), lax.rem(c + dc, n_rep)),
        ]
        pltpu.make_async_copy(ref, ref, c_recv.at[k, dx, dc]).wait()

    def loop(first, last, body):
        def step(k, carry):
            body(k)
            return carry

        lax.fori_loop(first, last, step, 0)

    loop(1, n_imp, lambda k: z_copy(k).start())

    imps[z] = imp_ref[...]
    eye = lax.broadcasted_iota(jnp.int32, (kpd, kpd), 0) == lax.broadcasted_iota(
        jnp.int32, (kpd, kpd), 1
    )
    my_caps = cap_ref[:, z * n_rep + c, :].astype(jnp.float32)
    log_caps = jnp.log2(0.25 * my_caps)
    for t in range(tiles):
        column = jnp.sum(jnp.where(eye, log_caps[t : t + 1, :], 0.0), axis=1, keepdims=True)
        cap_shift[t] = jnp.broadcast_to(column, (kpd, LANES))

    def code_of(b, s):
        return code_ref[b * per_tile + s]

    def store_lse(zz, rt, lane_block, value):
        owner = zz * nq + rt * (nq // rt_dev) + lane_block // rr
        at = lane_block % rr
        lse[owner, at : at + 1, :] = value

    def first_rows(zz):
        def one(rt, carry):
            b = zz * rt_dev + rt
            gains = []
            for s in range(per_tile):
                code = code_of(b, s)
                live = code < tiles
                gains.append((jnp.where(live, SCALE, 0.0), jnp.where(live, 0.0, LOWEST)))
                picked[s * kpd : (s + 1) * kpd, :] = camp_ref[
                    lax.rem(code, tiles), pl.ds(pl.multiple_of(c * kpd, kpd), kpd), :
                ]
            for offset in range(0, tile, span):
                found = imps[zz, pl.ds(pl.multiple_of(rt * tile + offset, span), span), :]
                affinity = lax.dot_general(
                    picked[...],
                    found,
                    (((1,), (1,)), ((), ())),
                    preferred_element_type=jnp.float32,
                )
                for s in range(per_tile):
                    gain, bias = gains[s]
                    scores[b, s * kpd : (s + 1) * kpd, offset : offset + span] = (
                        affinity[s * kpd : (s + 1) * kpd] * gain + bias
                    )
                for lane in range(offset, offset + span, LANES):
                    value = lse_sublanes(scores[b, :, lane : lane + LANES])
                    store_lse(zz, rt, lane // LANES, value)
            return carry

        lax.fori_loop(0, rt_dev, one, 0)

    def later_rows(b, carry):
        for s in range(per_tile):
            pair_shift[s * kpd : (s + 1) * kpd, :] = col_shift[lax.rem(code_of(b, s), tiles)]
        zz = lax.div(b, rt_dev)
        rt = lax.rem(b, rt_dev)
        for lane in range(0, tile, LANES):
            value = lse_sublanes(scores[b, :, lane : lane + LANES] + pair_shift[...])
            store_lse(zz, rt, lane // LANES, value)
        return carry

    def share_rows(it, row_own):
        def rs_copy(k):
            o = lax.rem(me + k, n)
            return pltpu.make_async_remote_copy(
                src_ref=lse.at[o],
                dst_ref=parts.at[it, me],
                send_sem=rs_send.at[o],
                recv_sem=rs_recv.at[me],
                device_id=device(o),
                device_id_type=MESH,
            )

        def rs_wait(k):
            o = lax.rem(me + k, n)
            pltpu.make_async_copy(parts.at[it, o], parts.at[it, o], rs_recv.at[o]).wait()

        def ag_copy(k):
            o = lax.rem(me + k, n)
            return pltpu.make_async_remote_copy(
                src_ref=rows.at[it, me],
                dst_ref=rows.at[it, me],
                send_sem=ag_send.at[o],
                recv_sem=ag_recv.at[me],
                device_id=device(o),
                device_id_type=MESH,
            )

        def ag_wait(k):
            o = lax.rem(me + k, n)
            pltpu.make_async_copy(rows.at[it, o], rows.at[it, o], ag_recv.at[o]).wait()

        loop(1, n, lambda k: rs_copy(k).start())
        parts[it, me] = lse[me]
        loop(1, n, rs_wait)
        everything = parts[it]
        high = jnp.max(everything, axis=0)
        total = high + jnp.log2(jnp.sum(jnp.exp2(everything - high[None]), axis=0))
        row_own = jnp.minimum(row_own, -total)
        rows[it, me] = row_own
        loop(1, n, lambda k: ag_copy(k).start())
        loop(1, n, lambda k: rs_copy(k).wait_send())
        loop(1, n, ag_wait)
        loop(1, n, lambda k: ag_copy(k).wait_send())
        return row_own

    lane_index = lax.broadcasted_iota(jnp.int32, (1, LANES), 1)

    def columns(it):
        chunk = min(32, kpd)
        pairs = n_imp * rt_dev * per_tile
        width = LANES
        groups = (pairs + width - 1) // width
        best = [jnp.full((kpd, LANES), LOWEST, jnp.float32) for _ in range(tiles)]
        sums = [jnp.zeros((kpd, LANES), jnp.float32) for _ in range(tiles)]
        for g in range(groups):
            first = g * width
            last = min(pairs, first + width)
            pair_shift[0:kpd, :] = jnp.full((kpd, LANES), LOWEST, jnp.float32)

            def one(b, tile_of):
                zz = lax.div(b, rt_dev)
                rt = lax.rem(b, rt_dev)
                shift = []
                for lane_block in range(tile // LANES):
                    owner = zz * nq + rt * (nq // rt_dev) + lane_block // rr
                    at = lane_block % rr
                    shift.append(rows[it, owner, at : at + 1, :])
                shift = jnp.concatenate(shift, axis=1)
                for s in range(per_tile):
                    here = lane_index == b * per_tile + s - first
                    tile_of = jnp.where(here, code_of(b, s), tile_of)
                    for k in range(0, kpd, chunk):
                        got = scores[b, s * kpd + k : s * kpd + k + chunk, :] + shift
                        high = jnp.max(got, axis=1, keepdims=True)
                        total = jnp.sum(jnp.exp2(got - high), axis=1, keepdims=True)
                        pair_shift[k : k + chunk, :] = jnp.where(
                            here, high + jnp.log2(total), pair_shift[k : k + chunk, :]
                        )
                return tile_of

            tile_of = lax.fori_loop(
                first // per_tile,
                last // per_tile,
                one,
                jnp.full((1, LANES), -1, jnp.int32),
            )
            found = pair_shift[0:kpd, :]
            for t in range(tiles):
                mine = jnp.where(tile_of == t, found, LOWEST)
                high = jnp.max(mine, axis=1, keepdims=True)
                new_best = jnp.maximum(best[t], high)
                fresh = jnp.sum(jnp.exp2(mine - new_best), axis=1, keepdims=True)
                if g == 0:
                    sums[t] = jnp.broadcast_to(fresh, (kpd, LANES))
                else:
                    sums[t] = sums[t] * jnp.exp2(best[t] - new_best) + fresh
                best[t] = new_best
        for t in range(tiles):
            old = col_shift[t] if it > 0 else jnp.zeros((kpd, LANES), jnp.float32)
            new = jnp.minimum(old, cap_shift[t] - (best[t] + jnp.log2(sums[t])))
            col_shift[t] = jnp.where(best[t] > NO_ROWS, new, old)

    first_rows(z)
    dcs = range(1, n_rep)
    dxs = range(1, n_camp)

    def forward_z(k):
        wait_z(k)
        for dx in dxs:
            x_copy(k, dx).start()
        for dc in dcs:
            c_copy(k, 0, dc).start()

    def forward_x(k):
        for dx in dxs:
            wait_x(k, dx)
            for dc in dcs:
                c_copy(k, dx, dc).start()

    def finish(k):
        for dx in range(n_camp):
            for dc in dcs:
                wait_c(k, dx, dc)
        first_rows(lax.rem(z + k, n_imp))

    forward_z(1)

    def pump(k):
        forward_z(k + 1)
        forward_x(k)
        finish(k)

    loop(1, n_imp - 1, pump)
    forward_x(n_imp - 1)
    finish(n_imp - 1)

    row_own = jnp.zeros((rr, LANES), jnp.float32)
    for it in range(ITERS):
        if it > 0:
            lax.fori_loop(0, n_imp * rt_dev, later_rows, 0)
        row_own = share_rows(it, row_own)
        columns(it)

    mine = z * n_rep + c
    n_col = n_imp * n_rep
    for t in range(tiles):
        flat = jnp.sum(
            jnp.where(eye, col_shift[t, :, 0:kpd], 0.0), axis=0, keepdims=True
        )
        cols[mine, t : t + 1, :] = flat * UNSCALE

    def out_copy(k):
        o = lax.rem(mine + k, n_col)
        return pltpu.make_async_remote_copy(
            src_ref=cols.at[mine],
            dst_ref=cols.at[mine],
            send_sem=out_send.at[o],
            recv_sem=out_recv.at[mine],
            device_id={"imp": lax.div(o, n_rep), "camp": x, "rep": lax.rem(o, n_rep)},
            device_id_type=MESH,
        )

    def out_wait(k):
        o = lax.rem(mine + k, n_col)
        pltpu.make_async_copy(cols.at[o], cols.at[o], out_recv.at[o]).wait()

    loop(1, n_col, lambda k: out_copy(k).start())
    for part in range(nq):
        row_out[part] = rows[ITERS - 1, z * nq + part] * UNSCALE

    def drain(k):
        z_copy(k).wait_send()
        for dx in dxs:
            x_copy(k, dx).wait_send()
        for dx in range(n_camp):
            for dc in dcs:
                c_copy(k, dx, dc).wait_send()

    loop(1, n_imp, drain)
    loop(1, n_col, out_wait)
    col_out[...] = cols[...]
    loop(1, n_col, lambda k: out_copy(k).wait_send())


def shards(n_imp, n_camp, n_rep, imp_embed, camp_embed, capacity, tile_lists, tile_counts):
    rt_dev, slots = tile_lists.shape[-2:]
    tiles = camp_embed.shape[0]
    tile = camp_embed.shape[1] * n_imp
    e = camp_embed.shape[2]
    kpd = tile // (n_imp * n_rep)
    nq = n_camp * n_rep
    n = n_imp * nq
    block = rt_dev * tile
    piece = block // nq
    rr = piece // LANES
    n_col = n_imp * n_rep
    per_tile = n_rep * slots
    lists = tile_lists.reshape(rt_dev, slots)
    counts = tile_counts.reshape(rt_dev)
    live = jnp.arange(slots, dtype=jnp.int32)[None, :] < counts[:, None]
    code = jnp.where(live, lists, lists + tiles)
    codes = lax.all_gather(code, ("imp", "rep"))
    codes = codes.reshape(n_imp, n_rep, rt_dev, slots).transpose(0, 2, 1, 3).reshape(-1)
    cfg = (n_imp, n_camp, n_rep, tiles, tile, rt_dev, slots)
    dma = pltpu.SemaphoreType.DMA
    vmem = pl.BlockSpec(memory_space=pltpu.VMEM)
    row_out, col_out = pl.pallas_call(
        functools.partial(kernel, cfg),
        out_shape=(
            jax.ShapeDtypeStruct((nq, rr, LANES), jnp.float32),
            jax.ShapeDtypeStruct((n_col, tiles, kpd), jnp.float32),
        ),
        in_specs=[pl.BlockSpec(memory_space=pltpu.SMEM), vmem, vmem, vmem],
        out_specs=(vmem, vmem),
        scratch_shapes=[
            pltpu.VMEM((n_imp, block, e), jnp.bfloat16),
            pltpu.VMEM((n_imp * rt_dev, per_tile * kpd, tile), jnp.float32),
            pltpu.VMEM((per_tile * kpd, e), jnp.bfloat16),
            pltpu.VMEM((n, rr, LANES), jnp.float32),
            pltpu.VMEM((ITERS, n, rr, LANES), jnp.float32),
            pltpu.VMEM((ITERS, n, rr, LANES), jnp.float32),
            pltpu.VMEM((tiles, kpd, LANES), jnp.float32),
            pltpu.VMEM((tiles, kpd, LANES), jnp.float32),
            pltpu.VMEM((per_tile * kpd, LANES), jnp.float32),
            pltpu.VMEM((n_col, tiles, kpd), jnp.float32),
            dma((n_imp,)),
            dma((n_imp,)),
            dma((n_imp, n_camp)),
            dma((n_imp, n_camp)),
            dma((n_imp, n_camp, n_rep)),
            dma((n_imp, n_camp, n_rep)),
            dma((n,)),
            dma((n,)),
            dma((n,)),
            dma((n,)),
            dma((n_col,)),
            dma((n_col,)),
        ],
        compiler_params=pltpu.CompilerParams(
            collective_id=0, has_side_effects=True, vmem_limit_bytes=56 * 1024 * 1024
        ),
    )(codes, imp_embed, camp_embed, capacity.reshape(tiles, n_col, kpd))
    return (row_out.reshape(-1), col_out.transpose(1, 0, 2).reshape(-1))


def solution(mesh):
    sizes = (mesh.shape["imp"], mesh.shape["camp"], mesh.shape["rep"])
    in_specs = (
        P(("groups", "imp"), None),
        P(("groups", "camp"), "imp", None),
        P(("groups", "camp")),
        P(("groups", "imp"), "camp", "rep", None, None),
        P(("groups", "imp"), "camp", "rep", None),
    )
    out_specs = (P(("groups", "imp")), P(("groups", "camp")))
    return jax.shard_map(
        functools.partial(shards, *sizes),
        mesh=mesh,
        in_specs=in_specs,
        out_specs=out_specs,
        check_vma=False,
    )
```

```python
import functools
import math

import jax
import jax.numpy as jnp
from jax import lax
from jax.experimental import pallas as pl
from jax.experimental.pallas import tpu as pltpu
from jax.sharding import PartitionSpec as P

ITERS = 2
LANES = 128
SCALE = 2.0 * math.log2(math.e)
UNSCALE = 1.0 / SCALE
LOWEST = -1e30
NO_ROWS = -1e29
MESH = pl.DeviceIdType.MESH


def lse_sublanes(x):
    high = jnp.max(x, axis=0, keepdims=True)
    return high + jnp.log2(jnp.sum(jnp.exp2(x - high), axis=0, keepdims=True))


def kernel(
    cfg,
    list_ref,
    count_ref,
    imp_ref,
    camp_ref,
    cap_ref,
    row_out,
    col_out,
    imps,
    scores,
    picked,
    lse,
    parts,
    rows,
    col_shift,
    cap_shift,
    pair_shift,
    cols,
    code_rows,
    codes,
    l_send,
    l_recv,
    l_sem,
    z_send,
    z_recv,
    x_send,
    x_recv,
    c_send,
    c_recv,
    rs_send,
    rs_recv,
    ag_send,
    ag_recv,
    out_send,
    out_recv,
):
    n_imp, n_camp, n_rep, tiles, tile, rt_dev, slots = cfg
    kpd = tile // (n_imp * n_rep)
    nq = n_camp * n_rep
    n = n_imp * nq
    block = rt_dev * tile
    piece = block // nq
    rr = piece // LANES
    per_tile = n_rep * slots
    span = min(256, tile)
    z = lax.axis_index("imp")
    x = lax.axis_index("camp")
    c = lax.axis_index("rep")
    me = z * nq + x * n_rep + c

    def device(o):
        oz = lax.div(o, nq)
        rest = lax.rem(o, nq)
        return {"imp": oz, "camp": lax.div(rest, n_rep), "rep": lax.rem(rest, n_rep)}

    barrier = pltpu.get_barrier_semaphore()

    def greet(k, carry):
        o = lax.rem(me + k, n)
        pl.semaphore_signal(barrier, inc=1, device_id=device(o), device_id_type=MESH)
        return carry

    lax.fori_loop(1, n, greet, 0)
    pl.semaphore_wait(barrier, n - 1)

    def piece_rows(ox, oc):
        return pl.ds(pl.multiple_of((ox * n_rep + oc) * piece, piece), piece)

    def block_at(side, step):
        return z - step if side == 0 else z + step

    def z_copy(side, step):
        at = block_at(side, step)
        src = imp_ref if isinstance(step, int) and step == 0 else imps.at[at]
        return pltpu.make_async_remote_copy(
            src_ref=src.at[piece_rows(x, c)],
            dst_ref=imps.at[at, piece_rows(x, c)],
            send_sem=z_send.at[side, step],
            recv_sem=z_recv.at[side, step + 1],
            device_id={"imp": z + 1 if side == 0 else z - 1, "camp": x, "rep": c},
            device_id_type=MESH,
        )

    def has_block(side, step):
        return z >= step if side == 0 else z + step < n_imp

    def has_next(side):
        return z + 1 < n_imp if side == 0 else z >= 1

    def x_copy(side, k, dx):
        ref = imps.at[block_at(side, k), piece_rows(x, c)]
        return pltpu.make_async_remote_copy(
            src_ref=ref,
            dst_ref=ref,
            send_sem=x_send.at[side, k, dx],
            recv_sem=x_recv.at[side, k, n_camp - dx],
            device_id={"imp": z, "camp": lax.rem(x + dx, n_camp), "rep": c},
            device_id_type=MESH,
        )

    def c_copy(side, k, dx, dc):
        ref = imps.at[block_at(side, k), piece_rows(lax.rem(x + dx, n_camp), c)]
        return pltpu.make_async_remote_copy(
            src_ref=ref,
            dst_ref=ref,
            send_sem=c_send.at[side, k, dx, dc],
            recv_sem=c_recv.at[side, k, dx, n_rep - dc],
            device_id={"imp": z, "camp": x, "rep": lax.rem(c + dc, n_rep)},
            device_id_type=MESH,
        )

    def wait_z(side, k):
        ref = imps.at[block_at(side, k), piece_rows(x, c)]
        pltpu.make_async_copy(ref, ref, z_recv.at[side, k]).wait()

    def wait_x(side, k, dx):
        ref = imps.at[block_at(side, k), piece_rows(lax.rem(x + dx, n_camp), c)]
        pltpu.make_async_copy(ref, ref, x_recv.at[side, k, dx]).wait()

    def wait_c(side, k, dx, dc):
        ref = imps.at[
            block_at(side, k),
            piece_rows(lax.rem(x + dx, n_camp), lax.rem(c + dc, n_rep)),
        ]
        pltpu.make_async_copy(ref, ref, c_recv.at[side, k, dx, dc]).wait()

    def loop(first, last, body):
        def step(k, carry):
            body(k)
            return carry

        lax.fori_loop(first, last, step, 0)

    mine = z * n_rep + c
    n_col = n_imp * n_rep
    lane_index = lax.broadcasted_iota(jnp.int32, (1, LANES), 1)
    code_row = jnp.zeros((1, LANES), jnp.int32)
    for rt in range(rt_dev):
        for s in range(slots):
            entry = list_ref[0, 0, 0, rt, s]
            entry = jnp.where(s < count_ref[0, 0, 0, rt], entry, entry + tiles)
            code_row = jnp.where(lane_index == rt * slots + s, entry, code_row)
    code_rows[mine] = code_row

    def list_copy(k):
        o = lax.rem(mine + k, n_col)
        return pltpu.make_async_remote_copy(
            src_ref=code_rows.at[mine],
            dst_ref=code_rows.at[mine],
            send_sem=l_send.at[o],
            recv_sem=l_recv.at[mine],
            device_id={"imp": lax.div(o, n_rep), "camp": x, "rep": lax.rem(o, n_rep)},
            device_id_type=MESH,
        )

    def list_wait(k):
        o = lax.rem(mine + k, n_col)
        pltpu.make_async_copy(code_rows.at[o], code_rows.at[o], l_recv.at[o]).wait()

    for side in range(2):

        @pl.when(has_next(side))
        def _(side=side):
            z_copy(side, 0).start()

    loop(1, n_col, lambda k: list_copy(k).start())

    imps[z] = imp_ref[...]
    eye = lax.broadcasted_iota(jnp.int32, (kpd, kpd), 0) == lax.broadcasted_iota(
        jnp.int32, (kpd, kpd), 1
    )
    my_caps = cap_ref[:, z * n_rep + c, :].astype(jnp.float32)
    log_caps = jnp.log2(0.25 * my_caps)
    for t in range(tiles):
        column = jnp.sum(jnp.where(eye, log_caps[t : t + 1, :], 0.0), axis=1, keepdims=True)
        cap_shift[t] = jnp.broadcast_to(column, (kpd, LANES))

    loop(1, n_col, list_wait)
    to_scalars = pltpu.make_async_copy(code_rows, codes, l_sem)
    to_scalars.start()
    to_scalars.wait()

    def code_of(b, s):
        zz = lax.div(b, rt_dev)
        return codes[zz * n_rep + s // slots, 0, lax.rem(b, rt_dev) * slots + s % slots]

    def store_lse(zz, rt, lane_block, value):
        owner = zz * nq + rt * (nq // rt_dev) + lane_block // rr
        at = lane_block % rr
        lse[owner, at : at + 1, :] = value

    def first_rows(zz):
        def one(rt, carry):
            b = zz * rt_dev + rt
            gains = []
            for s in range(per_tile):
                code = code_of(b, s)
                live = code < tiles
                gains.append((jnp.where(live, SCALE, 0.0), jnp.where(live, 0.0, LOWEST)))
                picked[s * kpd : (s + 1) * kpd, :] = camp_ref[
                    lax.rem(code, tiles), pl.ds(pl.multiple_of(c * kpd, kpd), kpd), :
                ]
            for offset in range(0, tile, span):
                found = imps[zz, pl.ds(pl.multiple_of(rt * tile + offset, span), span), :]
                affinity = lax.dot_general(
                    picked[...],
                    found,
                    (((1,), (1,)), ((), ())),
                    preferred_element_type=jnp.float32,
                )
                for s in range(per_tile):
                    gain, bias = gains[s]
                    scores[b, s * kpd : (s + 1) * kpd, offset : offset + span] = (
                        affinity[s * kpd : (s + 1) * kpd] * gain + bias
                    )
                for lane in range(offset, offset + span, LANES):
                    value = lse_sublanes(scores[b, :, lane : lane + LANES])
                    store_lse(zz, rt, lane // LANES, value)
            return carry

        lax.fori_loop(0, rt_dev, one, 0)

    def later_rows(b, carry):
        for s in range(per_tile):
            pair_shift[s * kpd : (s + 1) * kpd, :] = col_shift[lax.rem(code_of(b, s), tiles)]
        zz = lax.div(b, rt_dev)
        rt = lax.rem(b, rt_dev)
        for lane in range(0, tile, LANES):
            value = lse_sublanes(scores[b, :, lane : lane + LANES] + pair_shift[...])
            store_lse(zz, rt, lane // LANES, value)
        return carry

    def share_rows(it, row_own):
        def rs_copy(k):
            o = lax.rem(me + k, n)
            return pltpu.make_async_remote_copy(
                src_ref=lse.at[o],
                dst_ref=parts.at[it, me],
                send_sem=rs_send.at[o],
                recv_sem=rs_recv.at[me],
                device_id=device(o),
                device_id_type=MESH,
            )

        def rs_wait(k):
            o = lax.rem(me + k, n)
            pltpu.make_async_copy(parts.at[it, o], parts.at[it, o], rs_recv.at[o]).wait()

        def ag_copy(k):
            o = lax.rem(me + k, n)
            return pltpu.make_async_remote_copy(
                src_ref=rows.at[it, me],
                dst_ref=rows.at[it, me],
                send_sem=ag_send.at[o],
                recv_sem=ag_recv.at[me],
                device_id=device(o),
                device_id_type=MESH,
            )

        def ag_wait(k):
            o = lax.rem(me + k, n)
            pltpu.make_async_copy(rows.at[it, o], rows.at[it, o], ag_recv.at[o]).wait()

        loop(1, n, lambda k: rs_copy(k).start())
        parts[it, me] = lse[me]
        loop(1, n, rs_wait)
        everything = parts[it]
        high = jnp.max(everything, axis=0)
        total = high + jnp.log2(jnp.sum(jnp.exp2(everything - high[None]), axis=0))
        row_own = jnp.minimum(row_own, -total)
        rows[it, me] = row_own
        loop(1, n, lambda k: ag_copy(k).start())
        loop(1, n, lambda k: rs_copy(k).wait_send())
        loop(1, n, ag_wait)
        loop(1, n, lambda k: ag_copy(k).wait_send())
        return row_own

    def columns(it):
        chunk = min(32, kpd)
        pairs = n_imp * rt_dev * per_tile
        width = LANES
        groups = (pairs + width - 1) // width
        best = [jnp.full((kpd, LANES), LOWEST, jnp.float32) for _ in range(tiles)]
        sums = [jnp.zeros((kpd, LANES), jnp.float32) for _ in range(tiles)]
        for g in range(groups):
            first = g * width
            last = min(pairs, first + width)
            pair_shift[0:kpd, :] = jnp.full((kpd, LANES), LOWEST, jnp.float32)

            def one(b, tile_of):
                zz = lax.div(b, rt_dev)
                rt = lax.rem(b, rt_dev)
                shift = []
                for lane_block in range(tile // LANES):
                    owner = zz * nq + rt * (nq // rt_dev) + lane_block // rr
                    at = lane_block % rr
                    shift.append(rows[it, owner, at : at + 1, :])
                shift = jnp.concatenate(shift, axis=1)
                for s in range(per_tile):
                    here = lane_index == b * per_tile + s - first
                    tile_of = jnp.where(here, code_of(b, s), tile_of)
                    for k in range(0, kpd, chunk):
                        got = scores[b, s * kpd + k : s * kpd + k + chunk, :] + shift
                        high = jnp.max(got, axis=1, keepdims=True)
                        total = jnp.sum(jnp.exp2(got - high), axis=1, keepdims=True)
                        pair_shift[k : k + chunk, :] = jnp.where(
                            here, high + jnp.log2(total), pair_shift[k : k + chunk, :]
                        )
                return tile_of

            tile_of = lax.fori_loop(
                first // per_tile,
                last // per_tile,
                one,
                jnp.full((1, LANES), -1, jnp.int32),
            )
            found = pair_shift[0:kpd, :]
            for t in range(tiles):
                mine = jnp.where(tile_of == t, found, LOWEST)
                high = jnp.max(mine, axis=1, keepdims=True)
                new_best = jnp.maximum(best[t], high)
                fresh = jnp.sum(jnp.exp2(mine - new_best), axis=1, keepdims=True)
                if g == 0:
                    sums[t] = jnp.broadcast_to(fresh, (kpd, LANES))
                else:
                    sums[t] = sums[t] * jnp.exp2(best[t] - new_best) + fresh
                best[t] = new_best
        for t in range(tiles):
            old = col_shift[t] if it > 0 else jnp.zeros((kpd, LANES), jnp.float32)
            new = jnp.minimum(old, cap_shift[t] - (best[t] + jnp.log2(sums[t])))
            col_shift[t] = jnp.where(best[t] > NO_ROWS, new, old)

    first_rows(z)
    dcs = range(1, n_rep)
    dxs = range(1, n_camp)

    def forward_z(k):
        for side in range(2):

            @pl.when(has_block(side, k))
            def _(side=side):
                wait_z(side, k)

                @pl.when(has_next(side))
                def _():
                    z_copy(side, k).start()

                for dx in dxs:
                    x_copy(side, k, dx).start()
                for dc in dcs:
                    c_copy(side, k, 0, dc).start()

    def forward_x(k):
        for side in range(2):

            @pl.when(has_block(side, k))
            def _(side=side):
                for dx in dxs:
                    wait_x(side, k, dx)
                    for dc in dcs:
                        c_copy(side, k, dx, dc).start()

    def finish(k):
        for side in range(2):

            @pl.when(has_block(side, k))
            def _(side=side):
                for dx in range(n_camp):
                    for dc in dcs:
                        wait_c(side, k, dx, dc)
                first_rows(block_at(side, k))

    forward_z(1)

    def pump(k):
        forward_z(k + 1)
        forward_x(k)
        finish(k)

    loop(1, n_imp - 1, pump)
    forward_x(n_imp - 1)
    finish(n_imp - 1)

    row_own = jnp.zeros((rr, LANES), jnp.float32)
    for it in range(ITERS):
        if it > 0:
            lax.fori_loop(0, n_imp * rt_dev, later_rows, 0)
        row_own = share_rows(it, row_own)
        columns(it)

    for t in range(tiles):
        flat = jnp.sum(
            jnp.where(eye, col_shift[t, :, 0:kpd], 0.0), axis=0, keepdims=True
        )
        cols[mine, t : t + 1, :] = flat * UNSCALE

    def out_copy(k):
        o = lax.rem(mine + k, n_col)
        return pltpu.make_async_remote_copy(
            src_ref=cols.at[mine],
            dst_ref=cols.at[mine],
            send_sem=out_send.at[o],
            recv_sem=out_recv.at[mine],
            device_id={"imp": lax.div(o, n_rep), "camp": x, "rep": lax.rem(o, n_rep)},
            device_id_type=MESH,
        )

    def out_wait(k):
        o = lax.rem(mine + k, n_col)
        pltpu.make_async_copy(cols.at[o], cols.at[o], out_recv.at[o]).wait()

    loop(1, n_col, lambda k: out_copy(k).start())
    for part in range(nq):
        row_out[part] = rows[ITERS - 1, z * nq + part] * UNSCALE

    def drain(k):
        for side in range(2):

            @pl.when(has_block(side, k))
            def _(side=side):
                @pl.when(has_next(side))
                def _():
                    z_copy(side, k).wait_send()

                for dx in dxs:
                    x_copy(side, k, dx).wait_send()
                for dx in range(n_camp):
                    for dc in dcs:
                        c_copy(side, k, dx, dc).wait_send()

    for side in range(2):

        @pl.when(has_next(side))
        def _(side=side):
            z_copy(side, 0).wait_send()

    loop(1, n_imp, drain)
    loop(1, n_col, lambda k: list_copy(k).wait_send())
    loop(1, n_col, out_wait)
    for t in range(tiles):
        col_out[t] = cols[:, t, :]
    loop(1, n_col, lambda k: out_copy(k).wait_send())


def shards(n_imp, n_camp, n_rep, imp_embed, camp_embed, capacity, tile_lists, tile_counts):
    rt_dev, slots = tile_lists.shape[-2:]
    tiles = camp_embed.shape[0]
    tile = camp_embed.shape[1] * n_imp
    e = camp_embed.shape[2]
    kpd = tile // (n_imp * n_rep)
    nq = n_camp * n_rep
    n = n_imp * nq
    block = rt_dev * tile
    piece = block // nq
    rr = piece // LANES
    n_col = n_imp * n_rep
    per_tile = n_rep * slots
    cfg = (n_imp, n_camp, n_rep, tiles, tile, rt_dev, slots)
    dma = pltpu.SemaphoreType.DMA
    smem = pl.BlockSpec(memory_space=pltpu.SMEM)
    vmem = pl.BlockSpec(memory_space=pltpu.VMEM)
    row_out, col_out = pl.pallas_call(
        functools.partial(kernel, cfg),
        out_shape=(
            jax.ShapeDtypeStruct((nq, rr, LANES), jnp.float32),
            jax.ShapeDtypeStruct((tiles, n_col, kpd), jnp.float32),
        ),
        in_specs=[smem, smem, vmem, vmem, vmem],
        out_specs=(vmem, vmem),
        scratch_shapes=[
            pltpu.VMEM((n_imp, block, e), jnp.bfloat16),
            pltpu.VMEM((n_imp * rt_dev, per_tile * kpd, tile), jnp.float32),
            pltpu.VMEM((per_tile * kpd, e), jnp.bfloat16),
            pltpu.VMEM((n, rr, LANES), jnp.float32),
            pltpu.VMEM((ITERS, n, rr, LANES), jnp.float32),
            pltpu.VMEM((ITERS, n, rr, LANES), jnp.float32),
            pltpu.VMEM((tiles, kpd, LANES), jnp.float32),
            pltpu.VMEM((tiles, kpd, LANES), jnp.float32),
            pltpu.VMEM((per_tile * kpd, LANES), jnp.float32),
            pltpu.VMEM((n_col, tiles, kpd), jnp.float32),
            pltpu.VMEM((n_col, 1, LANES), jnp.int32),
            pltpu.SMEM((n_col, 1, LANES), jnp.int32),
            dma((n_col,)),
            dma((n_col,)),
            dma,
            dma((2, n_imp)),
            dma((2, n_imp)),
            dma((2, n_imp, n_camp)),
            dma((2, n_imp, n_camp)),
            dma((2, n_imp, n_camp, n_rep)),
            dma((2, n_imp, n_camp, n_rep)),
            dma((n,)),
            dma((n,)),
            dma((n,)),
            dma((n,)),
            dma((n_col,)),
            dma((n_col,)),
        ],
        compiler_params=pltpu.CompilerParams(
            collective_id=0, has_side_effects=True, vmem_limit_bytes=56 * 1024 * 1024
        ),
    )(tile_lists, tile_counts, imp_embed, camp_embed, capacity.reshape(tiles, n_col, kpd))
    return (row_out.reshape(-1), col_out.reshape(-1))


def solution(mesh):
    sizes = (mesh.shape["imp"], mesh.shape["camp"], mesh.shape["rep"])
    in_specs = (
        P(("groups", "imp"), None),
        P(("groups", "camp"), "imp", None),
        P(("groups", "camp")),
        P(("groups", "imp"), "camp", "rep", None, None),
        P(("groups", "imp"), "camp", "rep", None),
    )
    out_specs = (P(("groups", "imp")), P(("groups", "camp")))
    return jax.shard_map(
        functools.partial(shards, *sizes),
        mesh=mesh,
        in_specs=in_specs,
        out_specs=out_specs,
        check_vma=False,
    )
```

```python
import functools
import math

import jax
import jax.numpy as jnp
from jax import lax
from jax.experimental import pallas as pl
from jax.experimental.pallas import tpu as pltpu
from jax.sharding import PartitionSpec as P

ITERS = 2
LANES = 128
SCALE = 2.0 * math.log2(math.e)
UNSCALE = 1.0 / SCALE
LOWEST = -1e30
NO_ROWS = -1e29
MESH = pl.DeviceIdType.MESH


def lse_sublanes(x):
    high = jnp.max(x, axis=0, keepdims=True)
    return high + jnp.log2(jnp.sum(jnp.exp2(x - high), axis=0, keepdims=True))


def kernel(
    cfg,
    list_ref,
    count_ref,
    imp_ref,
    camp_ref,
    cap_ref,
    row_out,
    col_out,
    imps,
    scores,
    picked,
    lse,
    plane_parts,
    z_parts,
    rows,
    col_shift,
    cap_shift,
    pair_shift,
    cols,
    code_rows,
    codes,
    l_send,
    l_recv,
    lc_send,
    lc_recv,
    l_sem,
    z_send,
    z_recv,
    x_send,
    x_recv,
    c_send,
    c_recv,
    a_send,
    a_recv,
    b_send,
    b_recv,
    g_send,
    g_recv,
    o_send,
    o_recv,
    oc_send,
    oc_recv,
):
    n_imp, n_camp, n_rep, tiles, tile, rt_dev, slots = cfg
    kpd = tile // (n_imp * n_rep)
    nq = n_camp * n_rep
    block = rt_dev * tile
    piece = block // nq
    rr = piece // LANES
    per_tile = n_rep * slots
    span = min(256, tile)
    z = lax.axis_index("imp")
    x = lax.axis_index("camp")
    c = lax.axis_index("rep")
    q = x * n_rep + c

    def loop(first, last, body):
        if last - first <= 7:
            for k in range(first, last):
                body(k)
            return

        def step(k, carry):
            body(k)
            return carry

        lax.fori_loop(first, last, step, 0)

    def on_line(k):
        return {"imp": lax.rem(z + k, n_imp), "camp": x, "rep": c}

    def in_plane(k):
        o = lax.rem(q + k, nq)
        return {"imp": z, "camp": lax.div(o, n_rep), "rep": lax.rem(o, n_rep)}

    def on_chip(k):
        return {"imp": z, "camp": x, "rep": lax.rem(c + k, n_rep)}

    def share(buffer, send, recv, mine, count, target, source=None):
        def copy(k):
            return pltpu.make_async_remote_copy(
                src_ref=buffer.at[mine] if source is None else source(k),
                dst_ref=buffer.at[mine],
                send_sem=send.at[k],
                recv_sem=recv.at[count - k],
                device_id=target(k),
                device_id_type=MESH,
            )

        def wait(k):
            ref = buffer.at[lax.rem(mine + k, count)]
            pltpu.make_async_copy(ref, ref, recv.at[k]).wait()

        return (
            lambda: loop(1, count, lambda k: copy(k).start()),
            lambda: loop(1, count, wait),
            lambda: loop(1, count, lambda k: copy(k).wait_send()),
        )

    barrier = pltpu.get_barrier_semaphore()

    def greet(target):
        def signal(k):
            pl.semaphore_signal(barrier, inc=1, device_id=target(k), device_id_type=MESH)

        return signal

    loop(1, n_imp, greet(on_line))
    loop(1, nq, greet(in_plane))
    pl.semaphore_wait(barrier, n_imp + nq - 2)

    def piece_rows(ox, oc):
        return pl.ds(pl.multiple_of((ox * n_rep + oc) * piece, piece), piece)

    def block_at(side, step):
        return z - step if side == 0 else z + step

    def z_copy(side, step):
        at = block_at(side, step)
        src = imp_ref if isinstance(step, int) and step == 0 else imps.at[at]
        return pltpu.make_async_remote_copy(
            src_ref=src.at[piece_rows(x, c)],
            dst_ref=imps.at[at, piece_rows(x, c)],
            send_sem=z_send.at[side, step],
            recv_sem=z_recv.at[side, step + 1],
            device_id={"imp": z + 1 if side == 0 else z - 1, "camp": x, "rep": c},
            device_id_type=MESH,
        )

    def has_block(side, step):
        return z >= step if side == 0 else z + step < n_imp

    def has_next(side):
        return z + 1 < n_imp if side == 0 else z >= 1

    def x_copy(side, k, dx):
        ref = imps.at[block_at(side, k), piece_rows(x, c)]
        return pltpu.make_async_remote_copy(
            src_ref=ref,
            dst_ref=ref,
            send_sem=x_send.at[side, k, dx],
            recv_sem=x_recv.at[side, k, n_camp - dx],
            device_id={"imp": z, "camp": lax.rem(x + dx, n_camp), "rep": c},
            device_id_type=MESH,
        )

    def c_copy(side, k, dx, dc):
        ref = imps.at[block_at(side, k), piece_rows(lax.rem(x + dx, n_camp), c)]
        return pltpu.make_async_remote_copy(
            src_ref=ref,
            dst_ref=ref,
            send_sem=c_send.at[side, k, dx, dc],
            recv_sem=c_recv.at[side, k, dx, n_rep - dc],
            device_id={"imp": z, "camp": x, "rep": lax.rem(c + dc, n_rep)},
            device_id_type=MESH,
        )

    def wait_z(side, k):
        ref = imps.at[block_at(side, k), piece_rows(x, c)]
        pltpu.make_async_copy(ref, ref, z_recv.at[side, k]).wait()

    def wait_x(side, k, dx):
        ref = imps.at[block_at(side, k), piece_rows(lax.rem(x + dx, n_camp), c)]
        pltpu.make_async_copy(ref, ref, x_recv.at[side, k, dx]).wait()

    def wait_c(side, k, dx, dc):
        ref = imps.at[
            block_at(side, k),
            piece_rows(lax.rem(x + dx, n_camp), lax.rem(c + dc, n_rep)),
        ]
        pltpu.make_async_copy(ref, ref, c_recv.at[side, k, dx, dc]).wait()

    lane_index = lax.broadcasted_iota(jnp.int32, (1, LANES), 1)
    code_row = jnp.zeros((1, LANES), jnp.int32)
    for rt in range(rt_dev):
        for s in range(slots):
            entry = list_ref[0, 0, 0, rt, s]
            entry = jnp.where(s < count_ref[0, 0, 0, rt], entry, entry + tiles)
            code_row = jnp.where(lane_index == rt * slots + s, entry, code_row)
    code_rows[c, z] = code_row

    lists_go, lists_come, lists_left = share(
        code_rows.at[c], l_send, l_recv, z, n_imp, on_line
    )
    pairs_go, pairs_come, pairs_left = share(code_rows, lc_send, lc_recv, c, n_rep, on_chip)

    for side in range(2):

        @pl.when(has_next(side))
        def _(side=side):
            z_copy(side, 0).start()

    lists_go()

    imps[z] = imp_ref[...]
    eye = lax.broadcasted_iota(jnp.int32, (kpd, kpd), 0) == lax.broadcasted_iota(
        jnp.int32, (kpd, kpd), 1
    )
    my_caps = cap_ref[:, z * n_rep + c, :].astype(jnp.float32)
    log_caps = jnp.log2(0.25 * my_caps)
    for t in range(tiles):
        column = jnp.sum(jnp.where(eye, log_caps[t : t + 1, :], 0.0), axis=1, keepdims=True)
        cap_shift[t] = jnp.broadcast_to(column, (kpd, LANES))

    lists_come()
    pairs_go()
    pairs_come()
    to_scalars = pltpu.make_async_copy(code_rows, codes, l_sem)
    to_scalars.start()
    to_scalars.wait()

    def code_of(b, s):
        zz = lax.div(b, rt_dev)
        return codes[s // slots, zz, 0, lax.rem(b, rt_dev) * slots + s % slots]

    def store_lse(zz, rt, lane_block, value):
        owner = rt * (nq // rt_dev) + lane_block // rr
        at = lane_block % rr
        lse[owner, zz, at : at + 1, :] = value

    def first_rows(zz):
        def one(rt, carry):
            b = zz * rt_dev + rt
            gains = []
            for s in range(per_tile):
                code = code_of(b, s)
                live = code < tiles
                gains.append((jnp.where(live, SCALE, 0.0), jnp.where(live, 0.0, LOWEST)))
                picked[s * kpd : (s + 1) * kpd, :] = camp_ref[
                    lax.rem(code, tiles), pl.ds(pl.multiple_of(c * kpd, kpd), kpd), :
                ]
            for offset in range(0, tile, span):
                found = imps[zz, pl.ds(pl.multiple_of(rt * tile + offset, span), span), :]
                affinity = lax.dot_general(
                    picked[...],
                    found,
                    (((1,), (1,)), ((), ())),
                    preferred_element_type=jnp.float32,
                )
                for s in range(per_tile):
                    gain, bias = gains[s]
                    scores[b, s * kpd : (s + 1) * kpd, offset : offset + span] = (
                        affinity[s * kpd : (s + 1) * kpd] * gain + bias
                    )
                for lane in range(offset, offset + span, LANES):
                    value = lse_sublanes(scores[b, :, lane : lane + LANES])
                    store_lse(zz, rt, lane // LANES, value)
            return carry

        lax.fori_loop(0, rt_dev, one, 0)

    def later_rows(b, carry):
        for s in range(per_tile):
            pair_shift[s * kpd : (s + 1) * kpd, :] = col_shift[lax.rem(code_of(b, s), tiles)]
        zz = lax.div(b, rt_dev)
        rt = lax.rem(b, rt_dev)
        for lane in range(0, tile, LANES):
            value = lse_sublanes(scores[b, :, lane : lane + LANES] + pair_shift[...])
            store_lse(zz, rt, lane // LANES, value)
        return carry

    def merged(parts):
        high = jnp.max(parts, axis=0)
        return high + jnp.log2(jnp.sum(jnp.exp2(parts - high[None]), axis=0))

    def share_rows(it, row_own):
        go, come, left = share(
            plane_parts.at[it],
            a_send.at[it],
            a_recv.at[it],
            q,
            nq,
            in_plane,
            lambda k: lse.at[lax.rem(q + k, nq)],
        )
        go()
        plane_parts[it, q] = lse[q]
        come()
        z_parts[it, z] = merged(plane_parts[it])
        z_go, z_come, z_left = share(
            z_parts.at[it], b_send.at[it], b_recv.at[it], z, n_imp, on_line
        )
        z_go()
        left()
        z_come()
        row_own = jnp.minimum(row_own, -merged(z_parts[it]))
        rows[it, q] = row_own
        g_go, g_come, g_left = share(
            rows.at[it], g_send.at[it], g_recv.at[it], q, nq, in_plane
        )
        g_go()
        z_left()
        g_come()
        g_left()
        return row_own

    def columns(it):
        chunk = min(32, kpd)
        pairs = n_imp * rt_dev * per_tile
        width = LANES
        groups = (pairs + width - 1) // width
        best = [jnp.full((kpd, LANES), LOWEST, jnp.float32) for _ in range(tiles)]
        sums = [jnp.zeros((kpd, LANES), jnp.float32) for _ in range(tiles)]
        for g in range(groups):
            first = g * width
            last = min(pairs, first + width)
            pair_shift[0:kpd, :] = jnp.full((kpd, LANES), LOWEST, jnp.float32)

            def one(b, tile_of):
                zz = lax.div(b, rt_dev)
                rt = lax.rem(b, rt_dev)
                shift = []
                for lane_block in range(tile // LANES):
                    owner = rt * (nq // rt_dev) + lane_block // rr
                    at = lane_block % rr
                    shift.append(rows[it, owner, zz, at : at + 1, :])
                shift = jnp.concatenate(shift, axis=1)
                for s in range(per_tile):
                    here = lane_index == b * per_tile + s - first
                    tile_of = jnp.where(here, code_of(b, s), tile_of)
                    for k in range(0, kpd, chunk):
                        got = scores[b, s * kpd + k : s * kpd + k + chunk, :] + shift
                        high = jnp.max(got, axis=1, keepdims=True)
                        total = jnp.sum(jnp.exp2(got - high), axis=1, keepdims=True)
                        pair_shift[k : k + chunk, :] = jnp.where(
                            here, high + jnp.log2(total), pair_shift[k : k + chunk, :]
                        )
                return tile_of

            tile_of = lax.fori_loop(
                first // per_tile,
                last // per_tile,
                one,
                jnp.full((1, LANES), -1, jnp.int32),
            )
            found = pair_shift[0:kpd, :]
            for t in range(tiles):
                mine = jnp.where(tile_of == t, found, LOWEST)
                high = jnp.max(mine, axis=1, keepdims=True)
                new_best = jnp.maximum(best[t], high)
                fresh = jnp.sum(jnp.exp2(mine - new_best), axis=1, keepdims=True)
                if g == 0:
                    sums[t] = jnp.broadcast_to(fresh, (kpd, LANES))
                else:
                    sums[t] = sums[t] * jnp.exp2(best[t] - new_best) + fresh
                best[t] = new_best
        for t in range(tiles):
            old = col_shift[t] if it > 0 else jnp.zeros((kpd, LANES), jnp.float32)
            new = jnp.minimum(old, cap_shift[t] - (best[t] + jnp.log2(sums[t])))
            col_shift[t] = jnp.where(best[t] > NO_ROWS, new, old)

    first_rows(z)
    dcs = range(1, n_rep)
    dxs = range(1, n_camp)

    def forward_z(k):
        for side in range(2):

            @pl.when(has_block(side, k))
            def _(side=side):
                wait_z(side, k)

                @pl.when(has_next(side))
                def _():
                    z_copy(side, k).start()

                for dx in dxs:
                    x_copy(side, k, dx).start()
                for dc in dcs:
                    c_copy(side, k, 0, dc).start()

    def forward_x(k):
        for side in range(2):

            @pl.when(has_block(side, k))
            def _(side=side):
                for dx in dxs:
                    wait_x(side, k, dx)
                    for dc in dcs:
                        c_copy(side, k, dx, dc).start()

    def finish(k):
        for side in range(2):

            @pl.when(has_block(side, k))
            def _(side=side):
                for dx in range(n_camp):
                    for dc in dcs:
                        wait_c(side, k, dx, dc)
                first_rows(block_at(side, k))

    forward_z(1)

    def pump(k, carry):
        forward_z(k + 1)
        forward_x(k)
        finish(k)
        return carry

    lax.fori_loop(1, n_imp - 1, pump, 0)
    forward_x(n_imp - 1)
    finish(n_imp - 1)

    row_own = jnp.zeros((n_imp, rr, LANES), jnp.float32)
    for it in range(ITERS):
        if it > 0:
            lax.fori_loop(0, n_imp * rt_dev, later_rows, 0)
        row_own = share_rows(it, row_own)
        columns(it)

    for t in range(tiles):
        flat = jnp.sum(
            jnp.where(eye, col_shift[t, :, 0:kpd], 0.0), axis=0, keepdims=True
        )
        cols[c, z, t : t + 1, :] = flat * UNSCALE

    go, come, left = share(cols.at[c], o_send, o_recv, z, n_imp, on_line)
    c_go, c_come, c_left = share(cols, oc_send, oc_recv, c, n_rep, on_chip)
    go()
    for part in range(nq):
        row_out[part] = rows[ITERS - 1, part, z] * UNSCALE

    def drain(k):
        for side in range(2):

            @pl.when(has_block(side, k))
            def _(side=side):
                @pl.when(has_next(side))
                def _():
                    z_copy(side, k).wait_send()

                for dx in dxs:
                    x_copy(side, k, dx).wait_send()
                for dx in range(n_camp):
                    for dc in dcs:
                        c_copy(side, k, dx, dc).wait_send()

    for side in range(2):

        @pl.when(has_next(side))
        def _(side=side):
            z_copy(side, 0).wait_send()

    loop(1, n_imp, drain)
    lists_left()
    pairs_left()
    come()
    c_go()
    c_come()
    for oz in range(n_imp):
        for oc in range(n_rep):
            col_out[:, oz * n_rep + oc, :] = cols[oc, oz]
    left()
    c_left()


def shards(n_imp, n_camp, n_rep, imp_embed, camp_embed, capacity, tile_lists, tile_counts):
    rt_dev, slots = tile_lists.shape[-2:]
    tiles = camp_embed.shape[0]
    tile = camp_embed.shape[1] * n_imp
    e = camp_embed.shape[2]
    kpd = tile // (n_imp * n_rep)
    nq = n_camp * n_rep
    block = rt_dev * tile
    piece = block // nq
    rr = piece // LANES
    n_col = n_imp * n_rep
    per_tile = n_rep * slots
    cfg = (n_imp, n_camp, n_rep, tiles, tile, rt_dev, slots)
    dma = pltpu.SemaphoreType.DMA
    smem = pl.BlockSpec(memory_space=pltpu.SMEM)
    vmem = pl.BlockSpec(memory_space=pltpu.VMEM)
    row_out, col_out = pl.pallas_call(
        functools.partial(kernel, cfg),
        out_shape=(
            jax.ShapeDtypeStruct((nq, rr, LANES), jnp.float32),
            jax.ShapeDtypeStruct((tiles, n_col, kpd), jnp.float32),
        ),
        in_specs=[smem, smem, vmem, vmem, vmem],
        out_specs=(vmem, vmem),
        scratch_shapes=[
            pltpu.VMEM((n_imp, block, e), jnp.bfloat16),
            pltpu.VMEM((n_imp * rt_dev, per_tile * kpd, tile), jnp.float32),
            pltpu.VMEM((per_tile * kpd, e), jnp.bfloat16),
            pltpu.VMEM((nq, n_imp, rr, LANES), jnp.float32),
            pltpu.VMEM((ITERS, nq, n_imp, rr, LANES), jnp.float32),
            pltpu.VMEM((ITERS, n_imp, n_imp, rr, LANES), jnp.float32),
            pltpu.VMEM((ITERS, nq, n_imp, rr, LANES), jnp.float32),
            pltpu.VMEM((tiles, kpd, LANES), jnp.float32),
            pltpu.VMEM((tiles, kpd, LANES), jnp.float32),
            pltpu.VMEM((per_tile * kpd, LANES), jnp.float32),
            pltpu.VMEM((n_rep, n_imp, tiles, kpd), jnp.float32),
            pltpu.VMEM((n_rep, n_imp, 1, LANES), jnp.int32),
            pltpu.SMEM((n_rep, n_imp, 1, LANES), jnp.int32),
            dma((n_imp,)),
            dma((n_imp,)),
            dma((n_rep,)),
            dma((n_rep,)),
            dma,
            dma((2, n_imp)),
            dma((2, n_imp)),
            dma((2, n_imp, n_camp)),
            dma((2, n_imp, n_camp)),
            dma((2, n_imp, n_camp, n_rep)),
            dma((2, n_imp, n_camp, n_rep)),
            dma((ITERS, nq)),
            dma((ITERS, nq)),
            dma((ITERS, n_imp)),
            dma((ITERS, n_imp)),
            dma((ITERS, nq)),
            dma((ITERS, nq)),
            dma((n_imp,)),
            dma((n_imp,)),
            dma((n_rep,)),
            dma((n_rep,)),
        ],
        compiler_params=pltpu.CompilerParams(
            collective_id=0, has_side_effects=True, vmem_limit_bytes=56 * 1024 * 1024
        ),
    )(tile_lists, tile_counts, imp_embed, camp_embed, capacity.reshape(tiles, n_col, kpd))
    return (row_out.reshape(-1), col_out.reshape(-1))


def solution(mesh):
    sizes = (mesh.shape["imp"], mesh.shape["camp"], mesh.shape["rep"])
    in_specs = (
        P(("groups", "imp"), None),
        P(("groups", "camp"), "imp", None),
        P(("groups", "camp")),
        P(("groups", "imp"), "camp", "rep", None, None),
        P(("groups", "imp"), "camp", "rep", None),
    )
    out_specs = (P(("groups", "imp")), P(("groups", "camp")))
    return jax.shard_map(
        functools.partial(shards, *sizes),
        mesh=mesh,
        in_specs=in_specs,
        out_specs=out_specs,
        check_vma=False,
    )
```

```python
import functools
import math

import jax
import jax.numpy as jnp
from jax import lax
from jax.experimental import pallas as pl
from jax.experimental.pallas import tpu as pltpu
from jax.sharding import PartitionSpec as P

ITERS = 2
LANES = 128
SCALE = 2.0 * math.log2(math.e)
UNSCALE = 1.0 / SCALE
LOWEST = -1e30
NO_ROWS = -1e29
MESH = pl.DeviceIdType.MESH


def lse_sublanes(x):
    high = jnp.max(x, axis=0, keepdims=True)
    return high + jnp.log2(jnp.sum(jnp.exp2(x - high), axis=0, keepdims=True))


def kernel(
    cfg,
    list_ref,
    count_ref,
    imp_ref,
    camp_ref,
    cap_ref,
    row_out,
    col_out,
    imps,
    scores,
    picked,
    lse,
    parts,
    rows,
    col_shift,
    cap_shift,
    pair_shift,
    cols,
    code_rows,
    codes,
    l_send,
    l_recv,
    l_sem,
    z_send,
    z_recv,
    x_send,
    x_recv,
    c_send,
    c_recv,
    rs_send,
    rs_recv,
    ag_send,
    ag_recv,
    out_send,
    out_recv,
):
    n_imp, n_camp, n_rep, tiles, tile, rt_dev, slots = cfg
    kpd = tile // (n_imp * n_rep)
    nq = n_camp * n_rep
    n = n_imp * nq
    block = rt_dev * tile
    piece = block // nq
    rr = piece // LANES
    per_tile = n_rep * slots
    span = min(256, tile)
    z = lax.axis_index("imp")
    x = lax.axis_index("camp")
    c = lax.axis_index("rep")
    me = z * nq + x * n_rep + c

    def device(o):
        oz = lax.div(o, nq)
        rest = lax.rem(o, nq)
        return {"imp": oz, "camp": lax.div(rest, n_rep), "rep": lax.rem(rest, n_rep)}

    barrier = pltpu.get_barrier_semaphore()

    def greet(k, carry):
        o = lax.rem(me + k, n)
        pl.semaphore_signal(barrier, inc=1, device_id=device(o), device_id_type=MESH)
        return carry

    lax.fori_loop(1, n, greet, 0)
    pl.semaphore_wait(barrier, n - 1)

    def piece_rows(ox, oc):
        return pl.ds(pl.multiple_of((ox * n_rep + oc) * piece, piece), piece)

    def block_at(side, step):
        return z - step if side == 0 else z + step

    def z_copy(side, step):
        at = block_at(side, step)
        src = imp_ref if isinstance(step, int) and step == 0 else imps.at[at]
        return pltpu.make_async_remote_copy(
            src_ref=src.at[piece_rows(x, c)],
            dst_ref=imps.at[at, piece_rows(x, c)],
            send_sem=z_send.at[side, step],
            recv_sem=z_recv.at[side, step + 1],
            device_id={"imp": z + 1 if side == 0 else z - 1, "camp": x, "rep": c},
            device_id_type=MESH,
        )

    def has_block(side, step):
        return z >= step if side == 0 else z + step < n_imp

    def has_next(side):
        return z + 1 < n_imp if side == 0 else z >= 1

    def x_copy(side, k, dx):
        ref = imps.at[block_at(side, k), piece_rows(x, c)]
        return pltpu.make_async_remote_copy(
            src_ref=ref,
            dst_ref=ref,
            send_sem=x_send.at[side, k, dx],
            recv_sem=x_recv.at[side, k, n_camp - dx],
            device_id={"imp": z, "camp": lax.rem(x + dx, n_camp), "rep": c},
            device_id_type=MESH,
        )

    def c_copy(side, k, dx, dc):
        ref = imps.at[block_at(side, k), piece_rows(lax.rem(x + dx, n_camp), c)]
        return pltpu.make_async_remote_copy(
            src_ref=ref,
            dst_ref=ref,
            send_sem=c_send.at[side, k, dx, dc],
            recv_sem=c_recv.at[side, k, dx, n_rep - dc],
            device_id={"imp": z, "camp": x, "rep": lax.rem(c + dc, n_rep)},
            device_id_type=MESH,
        )

    def wait_z(side, k):
        ref = imps.at[block_at(side, k), piece_rows(x, c)]
        pltpu.make_async_copy(ref, ref, z_recv.at[side, k]).wait()

    def wait_x(side, k, dx):
        ref = imps.at[block_at(side, k), piece_rows(lax.rem(x + dx, n_camp), c)]
        pltpu.make_async_copy(ref, ref, x_recv.at[side, k, dx]).wait()

    def wait_c(side, k, dx, dc):
        ref = imps.at[
            block_at(side, k),
            piece_rows(lax.rem(x + dx, n_camp), lax.rem(c + dc, n_rep)),
        ]
        pltpu.make_async_copy(ref, ref, c_recv.at[side, k, dx, dc]).wait()

    def loop(first, last, body):
        def step(k, carry):
            body(k)
            return carry

        lax.fori_loop(first, last, step, 0)

    mine = z * n_rep + c
    n_col = n_imp * n_rep
    lane_index = lax.broadcasted_iota(jnp.int32, (1, LANES), 1)
    code_row = jnp.zeros((1, LANES), jnp.int32)
    for rt in range(rt_dev):
        for s in range(slots):
            entry = list_ref[0, 0, 0, rt, s]
            entry = jnp.where(s < count_ref[0, 0, 0, rt], entry, entry + tiles)
            code_row = jnp.where(lane_index == rt * slots + s, entry, code_row)
    code_rows[mine] = code_row

    def list_copy(k):
        o = lax.rem(mine + k, n_col)
        return pltpu.make_async_remote_copy(
            src_ref=code_rows.at[mine],
            dst_ref=code_rows.at[mine],
            send_sem=l_send.at[o],
            recv_sem=l_recv.at[mine],
            device_id={"imp": lax.div(o, n_rep), "camp": x, "rep": lax.rem(o, n_rep)},
            device_id_type=MESH,
        )

    def list_wait(k):
        o = lax.rem(mine + k, n_col)
        pltpu.make_async_copy(code_rows.at[o], code_rows.at[o], l_recv.at[o]).wait()

    for side in range(2):

        @pl.when(has_next(side))
        def _(side=side):
            z_copy(side, 0).start()

    loop(1, n_col, lambda k: list_copy(k).start())

    imps[z] = imp_ref[...]
    eye = lax.broadcasted_iota(jnp.int32, (kpd, kpd), 0) == lax.broadcasted_iota(
        jnp.int32, (kpd, kpd), 1
    )
    my_caps = cap_ref[:, z * n_rep + c, :].astype(jnp.float32)
    log_caps = jnp.log2(0.25 * my_caps)
    for t in range(tiles):
        column = jnp.sum(jnp.where(eye, log_caps[t : t + 1, :], 0.0), axis=1, keepdims=True)
        cap_shift[t] = jnp.broadcast_to(column, (kpd, LANES))

    loop(1, n_col, list_wait)
    to_scalars = pltpu.make_async_copy(code_rows, codes, l_sem)
    to_scalars.start()
    to_scalars.wait()

    def code_of(b, s):
        zz = lax.div(b, rt_dev)
        return codes[zz * n_rep + s // slots, 0, lax.rem(b, rt_dev) * slots + s % slots]

    def store_lse(zz, rt, lane_block, value):
        owner = zz * nq + rt * (nq // rt_dev) + lane_block // rr
        at = lane_block % rr
        lse[owner, at : at + 1, :] = value

    def rs_copy(it, o):
        return pltpu.make_async_remote_copy(
            src_ref=lse.at[o],
            dst_ref=parts.at[it, me],
            send_sem=rs_send.at[o],
            recv_sem=rs_recv.at[me],
            device_id=device(o),
            device_id_type=MESH,
        )

    def send_block(it, zz):
        for part in range(nq):
            o = zz * nq + part

            @pl.when(o != me)
            def _(o=o):
                rs_copy(it, o).start()

    def first_rows(zz):
        def one(rt, carry):
            b = zz * rt_dev + rt
            gains = []
            for s in range(per_tile):
                code = code_of(b, s)
                live = code < tiles
                gains.append((jnp.where(live, SCALE, 0.0), jnp.where(live, 0.0, LOWEST)))
                picked[s * kpd : (s + 1) * kpd, :] = camp_ref[
                    lax.rem(code, tiles), pl.ds(pl.multiple_of(c * kpd, kpd), kpd), :
                ]
            for offset in range(0, tile, span):
                found = imps[zz, pl.ds(pl.multiple_of(rt * tile + offset, span), span), :]
                affinity = lax.dot_general(
                    picked[...],
                    found,
                    (((1,), (1,)), ((), ())),
                    preferred_element_type=jnp.float32,
                )
                for s in range(per_tile):
                    gain, bias = gains[s]
                    scores[b, s * kpd : (s + 1) * kpd, offset : offset + span] = (
                        affinity[s * kpd : (s + 1) * kpd] * gain + bias
                    )
                for lane in range(offset, offset + span, LANES):
                    value = lse_sublanes(scores[b, :, lane : lane + LANES])
                    store_lse(zz, rt, lane // LANES, value)
            return carry

        lax.fori_loop(0, rt_dev, one, 0)
        send_block(0, zz)

    def later_rows(b):
        for s in range(per_tile):
            pair_shift[s * kpd : (s + 1) * kpd, :] = col_shift[lax.rem(code_of(b, s), tiles)]
        zz = lax.div(b, rt_dev)
        rt = lax.rem(b, rt_dev)
        for lane in range(0, tile, LANES):
            value = lse_sublanes(scores[b, :, lane : lane + LANES] + pair_shift[...])
            store_lse(zz, rt, lane // LANES, value)

    def ag_copy(it, k):
        o = lax.rem(me + k, n)
        return pltpu.make_async_remote_copy(
            src_ref=rows.at[it, me],
            dst_ref=rows.at[it, me],
            send_sem=ag_send.at[o],
            recv_sem=ag_recv.at[me],
            device_id=device(o),
            device_id_type=MESH,
        )

    def wait_block(it, zz):
        for part in range(nq):
            o = zz * nq + part

            @pl.when(o != me)
            def _(o=o):
                pltpu.make_async_copy(rows.at[it, o], rows.at[it, o], ag_recv.at[o]).wait()

    def share_rows(it, row_own):
        def rs_wait(k):
            o = lax.rem(me + k, n)
            pltpu.make_async_copy(parts.at[it, o], parts.at[it, o], rs_recv.at[o]).wait()

        parts[it, me] = lse[me]
        loop(1, n, rs_wait)
        everything = parts[it]
        high = jnp.max(everything, axis=0)
        total = high + jnp.log2(jnp.sum(jnp.exp2(everything - high[None]), axis=0))
        row_own = jnp.minimum(row_own, -total)
        rows[it, me] = row_own
        loop(1, n, lambda k: ag_copy(it, k).start())
        loop(1, n, lambda k: rs_copy(it, lax.rem(me + k, n)).wait_send())
        return row_own

    def columns(it):
        chunk = min(32, kpd)
        pairs = n_imp * rt_dev * per_tile
        width = LANES
        groups = (pairs + width - 1) // width
        best = [jnp.full((kpd, LANES), LOWEST, jnp.float32) for _ in range(tiles)]
        sums = [jnp.zeros((kpd, LANES), jnp.float32) for _ in range(tiles)]
        for g in range(groups):
            first = g * width
            last = min(pairs, first + width)
            pair_shift[0:kpd, :] = jnp.full((kpd, LANES), LOWEST, jnp.float32)

            def one(at_b, tile_of):
                b = lax.rem(z * rt_dev + at_b, n_imp * rt_dev)
                zz = lax.div(b, rt_dev)
                rt = lax.rem(b, rt_dev)

                @pl.when(rt == 0)
                def _():
                    wait_block(it, zz)

                shift = []
                for lane_block in range(tile // LANES):
                    owner = zz * nq + rt * (nq // rt_dev) + lane_block // rr
                    at = lane_block % rr
                    shift.append(rows[it, owner, at : at + 1, :])
                shift = jnp.concatenate(shift, axis=1)
                for s in range(per_tile):
                    here = lane_index == at_b * per_tile + s - first
                    tile_of = jnp.where(here, code_of(b, s), tile_of)
                    for k in range(0, kpd, chunk):
                        got = scores[b, s * kpd + k : s * kpd + k + chunk, :] + shift
                        high = jnp.max(got, axis=1, keepdims=True)
                        total = jnp.sum(jnp.exp2(got - high), axis=1, keepdims=True)
                        pair_shift[k : k + chunk, :] = jnp.where(
                            here, high + jnp.log2(total), pair_shift[k : k + chunk, :]
                        )
                return tile_of

            tile_of = lax.fori_loop(
                first // per_tile,
                last // per_tile,
                one,
                jnp.full((1, LANES), -1, jnp.int32),
            )
            found = pair_shift[0:kpd, :]
            for t in range(tiles):
                mine = jnp.where(tile_of == t, found, LOWEST)
                high = jnp.max(mine, axis=1, keepdims=True)
                new_best = jnp.maximum(best[t], high)
                fresh = jnp.sum(jnp.exp2(mine - new_best), axis=1, keepdims=True)
                if g == 0:
                    sums[t] = jnp.broadcast_to(fresh, (kpd, LANES))
                else:
                    sums[t] = sums[t] * jnp.exp2(best[t] - new_best) + fresh
                best[t] = new_best
        for t in range(tiles):
            old = col_shift[t] if it > 0 else jnp.zeros((kpd, LANES), jnp.float32)
            new = jnp.minimum(old, cap_shift[t] - (best[t] + jnp.log2(sums[t])))
            col_shift[t] = jnp.where(best[t] > NO_ROWS, new, old)

    first_rows(z)
    dcs = range(1, n_rep)
    dxs = range(1, n_camp)

    def forward_z(k):
        for side in range(2):

            @pl.when(has_block(side, k))
            def _(side=side):
                wait_z(side, k)

                @pl.when(has_next(side))
                def _():
                    z_copy(side, k).start()

                for dx in dxs:
                    x_copy(side, k, dx).start()
                for dc in dcs:
                    c_copy(side, k, 0, dc).start()

    def forward_x(k):
        for side in range(2):

            @pl.when(has_block(side, k))
            def _(side=side):
                for dx in dxs:
                    wait_x(side, k, dx)
                    for dc in dcs:
                        c_copy(side, k, dx, dc).start()

    def finish(k):
        for side in range(2):

            @pl.when(has_block(side, k))
            def _(side=side):
                for dx in range(n_camp):
                    for dc in dcs:
                        wait_c(side, k, dx, dc)
                first_rows(block_at(side, k))

    forward_z(1)

    def pump(k):
        forward_z(k + 1)
        forward_x(k)
        finish(k)

    loop(1, n_imp - 1, pump)
    forward_x(n_imp - 1)
    finish(n_imp - 1)

    row_own = jnp.zeros((rr, LANES), jnp.float32)
    for it in range(ITERS):
        if it > 0:

            def later_block(k):
                zz = lax.rem(z + 1 + k, n_imp)
                loop(0, rt_dev, lambda rt: later_rows(zz * rt_dev + rt))
                send_block(1, zz)

            loop(0, n_imp, later_block)
        row_own = share_rows(it, row_own)
        columns(it)
        loop(1, n, lambda k: ag_copy(it, k).wait_send())

    for t in range(tiles):
        flat = jnp.sum(
            jnp.where(eye, col_shift[t, :, 0:kpd], 0.0), axis=0, keepdims=True
        )
        cols[mine, t : t + 1, :] = flat * UNSCALE

    def out_copy(k):
        o = lax.rem(mine + k, n_col)
        return pltpu.make_async_remote_copy(
            src_ref=cols.at[mine],
            dst_ref=cols.at[mine],
            send_sem=out_send.at[o],
            recv_sem=out_recv.at[mine],
            device_id={"imp": lax.div(o, n_rep), "camp": x, "rep": lax.rem(o, n_rep)},
            device_id_type=MESH,
        )

    def out_wait(k):
        o = lax.rem(mine + k, n_col)
        pltpu.make_async_copy(cols.at[o], cols.at[o], out_recv.at[o]).wait()

    loop(1, n_col, lambda k: out_copy(k).start())
    for part in range(nq):
        row_out[part] = rows[ITERS - 1, z * nq + part] * UNSCALE

    def drain(k):
        for side in range(2):

            @pl.when(has_block(side, k))
            def _(side=side):
                @pl.when(has_next(side))
                def _():
                    z_copy(side, k).wait_send()

                for dx in dxs:
                    x_copy(side, k, dx).wait_send()
                for dx in range(n_camp):
                    for dc in dcs:
                        c_copy(side, k, dx, dc).wait_send()

    for side in range(2):

        @pl.when(has_next(side))
        def _(side=side):
            z_copy(side, 0).wait_send()

    loop(1, n_imp, drain)
    loop(1, n_col, lambda k: list_copy(k).wait_send())
    loop(1, n_col, out_wait)
    for t in range(tiles):
        col_out[t] = cols[:, t, :]
    loop(1, n_col, lambda k: out_copy(k).wait_send())


def shards(n_imp, n_camp, n_rep, imp_embed, camp_embed, capacity, tile_lists, tile_counts):
    rt_dev, slots = tile_lists.shape[-2:]
    tiles = camp_embed.shape[0]
    tile = camp_embed.shape[1] * n_imp
    e = camp_embed.shape[2]
    kpd = tile // (n_imp * n_rep)
    nq = n_camp * n_rep
    n = n_imp * nq
    block = rt_dev * tile
    piece = block // nq
    rr = piece // LANES
    n_col = n_imp * n_rep
    per_tile = n_rep * slots
    cfg = (n_imp, n_camp, n_rep, tiles, tile, rt_dev, slots)
    dma = pltpu.SemaphoreType.DMA
    smem = pl.BlockSpec(memory_space=pltpu.SMEM)
    vmem = pl.BlockSpec(memory_space=pltpu.VMEM)
    row_out, col_out = pl.pallas_call(
        functools.partial(kernel, cfg),
        out_shape=(
            jax.ShapeDtypeStruct((nq, rr, LANES), jnp.float32),
            jax.ShapeDtypeStruct((tiles, n_col, kpd), jnp.float32),
        ),
        in_specs=[smem, smem, vmem, vmem, vmem],
        out_specs=(vmem, vmem),
        scratch_shapes=[
            pltpu.VMEM((n_imp, block, e), jnp.bfloat16),
            pltpu.VMEM((n_imp * rt_dev, per_tile * kpd, tile), jnp.float32),
            pltpu.VMEM((per_tile * kpd, e), jnp.bfloat16),
            pltpu.VMEM((n, rr, LANES), jnp.float32),
            pltpu.VMEM((ITERS, n, rr, LANES), jnp.float32),
            pltpu.VMEM((ITERS, n, rr, LANES), jnp.float32),
            pltpu.VMEM((tiles, kpd, LANES), jnp.float32),
            pltpu.VMEM((tiles, kpd, LANES), jnp.float32),
            pltpu.VMEM((per_tile * kpd, LANES), jnp.float32),
            pltpu.VMEM((n_col, tiles, kpd), jnp.float32),
            pltpu.VMEM((n_col, 1, LANES), jnp.int32),
            pltpu.SMEM((n_col, 1, LANES), jnp.int32),
            dma((n_col,)),
            dma((n_col,)),
            dma,
            dma((2, n_imp)),
            dma((2, n_imp)),
            dma((2, n_imp, n_camp)),
            dma((2, n_imp, n_camp)),
            dma((2, n_imp, n_camp, n_rep)),
            dma((2, n_imp, n_camp, n_rep)),
            dma((n,)),
            dma((n,)),
            dma((n,)),
            dma((n,)),
            dma((n_col,)),
            dma((n_col,)),
        ],
        compiler_params=pltpu.CompilerParams(
            collective_id=0, has_side_effects=True, vmem_limit_bytes=56 * 1024 * 1024
        ),
    )(tile_lists, tile_counts, imp_embed, camp_embed, capacity.reshape(tiles, n_col, kpd))
    return (row_out.reshape(-1), col_out.reshape(-1))


def solution(mesh):
    sizes = (mesh.shape["imp"], mesh.shape["camp"], mesh.shape["rep"])
    in_specs = (
        P(("groups", "imp"), None),
        P(("groups", "camp"), "imp", None),
        P(("groups", "camp")),
        P(("groups", "imp"), "camp", "rep", None, None),
        P(("groups", "imp"), "camp", "rep", None),
    )
    out_specs = (P(("groups", "imp")), P(("groups", "camp")))
    return jax.shard_map(
        functools.partial(shards, *sizes),
        mesh=mesh,
        in_specs=in_specs,
        out_specs=out_specs,
        check_vma=False,
    )
```

```python
import functools
import math

import jax
import jax.numpy as jnp
from jax import lax
from jax.experimental import pallas as pl
from jax.experimental.pallas import tpu as pltpu
from jax.sharding import PartitionSpec as P

ITERS = 2
LANES = 128
SCALE = 2.0 * math.log2(math.e)
UNSCALE = 1.0 / SCALE
LOWEST = -1e30
NO_ROWS = -1e29
MESH = pl.DeviceIdType.MESH


def lse_sublanes(x):
    high = jnp.max(x, axis=0, keepdims=True)
    return high + jnp.log2(jnp.sum(jnp.exp2(x - high), axis=0, keepdims=True))


def kernel(
    cfg,
    list_ref,
    count_ref,
    imp_ref,
    camp_ref,
    cap_ref,
    row_out,
    col_out,
    imps,
    scores,
    picked,
    lse,
    parts,
    rows,
    col_shift,
    cap_shift,
    pair_shift,
    cols,
    code_rows,
    codes,
    l_send,
    l_recv,
    l_sem,
    z_send,
    z_recv,
    x_send,
    x_recv,
    c_send,
    c_recv,
    rs_send,
    rs_recv,
    ag_send,
    ag_recv,
    out_send,
    out_recv,
):
    n_imp, n_camp, n_rep, tiles, tile, rt_dev, slots = cfg
    kpd = tile // (n_imp * n_rep)
    nq = n_camp * n_rep
    n = n_imp * nq
    block = rt_dev * tile
    piece = block // nq
    rr = piece // LANES
    per_tile = n_rep * slots
    span = min(256, tile)
    z = lax.axis_index("imp")
    x = lax.axis_index("camp")
    c = lax.axis_index("rep")
    me = z * nq + x * n_rep + c

    def device(o):
        oz = lax.div(o, nq)
        rest = lax.rem(o, nq)
        return {"imp": oz, "camp": lax.div(rest, n_rep), "rep": lax.rem(rest, n_rep)}

    barrier = pltpu.get_barrier_semaphore()

    def greet(k, carry):
        o = lax.rem(me + k, n)
        pl.semaphore_signal(barrier, inc=1, device_id=device(o), device_id_type=MESH)
        return carry

    lax.fori_loop(1, n, greet, 0)
    pl.semaphore_wait(barrier, n - 1)

    def piece_rows(ox, oc):
        return pl.ds(pl.multiple_of((ox * n_rep + oc) * piece, piece), piece)

    def block_at(side, step):
        return z - step if side == 0 else z + step

    def z_copy(side, step):
        at = block_at(side, step)
        src = imp_ref if isinstance(step, int) and step == 0 else imps.at[at]
        return pltpu.make_async_remote_copy(
            src_ref=src.at[piece_rows(x, c)],
            dst_ref=imps.at[at, piece_rows(x, c)],
            send_sem=z_send.at[side, step],
            recv_sem=z_recv.at[side, step + 1],
            device_id={"imp": z + 1 if side == 0 else z - 1, "camp": x, "rep": c},
            device_id_type=MESH,
        )

    def has_block(side, step):
        return z >= step if side == 0 else z + step < n_imp

    def has_next(side):
        return z + 1 < n_imp if side == 0 else z >= 1

    def x_copy(side, k, dx):
        ref = imps.at[block_at(side, k), piece_rows(x, c)]
        return pltpu.make_async_remote_copy(
            src_ref=ref,
            dst_ref=ref,
            send_sem=x_send.at[side, k, dx],
            recv_sem=x_recv.at[side, k, n_camp - dx],
            device_id={"imp": z, "camp": lax.rem(x + dx, n_camp), "rep": c},
            device_id_type=MESH,
        )

    def c_copy(side, k, dx, dc):
        ref = imps.at[block_at(side, k), piece_rows(lax.rem(x + dx, n_camp), c)]
        return pltpu.make_async_remote_copy(
            src_ref=ref,
            dst_ref=ref,
            send_sem=c_send.at[side, k, dx, dc],
            recv_sem=c_recv.at[side, k, dx, n_rep - dc],
            device_id={"imp": z, "camp": x, "rep": lax.rem(c + dc, n_rep)},
            device_id_type=MESH,
        )

    def wait_z(side, k):
        ref = imps.at[block_at(side, k), piece_rows(x, c)]
        pltpu.make_async_copy(ref, ref, z_recv.at[side, k]).wait()

    def wait_x(side, k, dx):
        ref = imps.at[block_at(side, k), piece_rows(lax.rem(x + dx, n_camp), c)]
        pltpu.make_async_copy(ref, ref, x_recv.at[side, k, dx]).wait()

    def wait_c(side, k, dx, dc):
        ref = imps.at[
            block_at(side, k),
            piece_rows(lax.rem(x + dx, n_camp), lax.rem(c + dc, n_rep)),
        ]
        pltpu.make_async_copy(ref, ref, c_recv.at[side, k, dx, dc]).wait()

    def sends(first, last, body):
        if last - first > 15:
            loop(first, last, body)
            return
        for k in range(first, last):
            body(k)

    def loop(first, last, body):
        def step(k, carry):
            body(k)
            return carry

        lax.fori_loop(first, last, step, 0)

    mine = z * n_rep + c
    n_col = n_imp * n_rep
    lane_index = lax.broadcasted_iota(jnp.int32, (1, LANES), 1)
    code_row = jnp.zeros((1, LANES), jnp.int32)
    for rt in range(rt_dev):
        for s in range(slots):
            entry = list_ref[0, 0, 0, rt, s]
            entry = jnp.where(s < count_ref[0, 0, 0, rt], entry, entry + tiles)
            code_row = jnp.where(lane_index == rt * slots + s, entry, code_row)
    code_rows[mine] = code_row

    def list_copy(k):
        o = lax.rem(mine + k, n_col)
        return pltpu.make_async_remote_copy(
            src_ref=code_rows.at[mine],
            dst_ref=code_rows.at[mine],
            send_sem=l_send.at[o],
            recv_sem=l_recv.at[mine],
            device_id={"imp": lax.div(o, n_rep), "camp": x, "rep": lax.rem(o, n_rep)},
            device_id_type=MESH,
        )

    def list_wait(k):
        o = lax.rem(mine + k, n_col)
        pltpu.make_async_copy(code_rows.at[o], code_rows.at[o], l_recv.at[o]).wait()

    for side in range(2):

        @pl.when(has_next(side))
        def _(side=side):
            z_copy(side, 0).start()

    sends(1, n_col, lambda k: list_copy(k).start())

    imps[z] = imp_ref[...]
    eye = lax.broadcasted_iota(jnp.int32, (kpd, kpd), 0) == lax.broadcasted_iota(
        jnp.int32, (kpd, kpd), 1
    )
    my_caps = cap_ref[:, z * n_rep + c, :].astype(jnp.float32)
    log_caps = jnp.log2(0.25 * my_caps)
    for t in range(tiles):
        column = jnp.sum(jnp.where(eye, log_caps[t : t + 1, :], 0.0), axis=1, keepdims=True)
        cap_shift[t] = jnp.broadcast_to(column, (kpd, LANES))

    loop(1, n_col, list_wait)
    to_scalars = pltpu.make_async_copy(code_rows, codes, l_sem)
    to_scalars.start()
    to_scalars.wait()

    def code_of(b, s):
        zz = lax.div(b, rt_dev)
        return codes[zz * n_rep + s // slots, 0, lax.rem(b, rt_dev) * slots + s % slots]

    def store_lse(zz, rt, lane_block, value):
        owner = zz * nq + rt * (nq // rt_dev) + lane_block // rr
        at = lane_block % rr
        lse[owner, at : at + 1, :] = value

    def rs_copy(it, o):
        return pltpu.make_async_remote_copy(
            src_ref=lse.at[o],
            dst_ref=parts.at[it, me],
            send_sem=rs_send.at[o],
            recv_sem=rs_recv.at[me],
            device_id=device(o),
            device_id_type=MESH,
        )

    def send_block(it, zz):
        for part in range(nq):
            o = zz * nq + part

            @pl.when(o != me)
            def _(o=o):
                rs_copy(it, o).start()

    def first_rows(zz):
        def one(rt, carry):
            b = zz * rt_dev + rt
            gains = []
            for s in range(per_tile):
                code = code_of(b, s)
                live = code < tiles
                gains.append((jnp.where(live, SCALE, 0.0), jnp.where(live, 0.0, LOWEST)))
                picked[s * kpd : (s + 1) * kpd, :] = camp_ref[
                    lax.rem(code, tiles), pl.ds(pl.multiple_of(c * kpd, kpd), kpd), :
                ]
            for offset in range(0, tile, span):
                found = imps[zz, pl.ds(pl.multiple_of(rt * tile + offset, span), span), :]
                affinity = lax.dot_general(
                    picked[...],
                    found,
                    (((1,), (1,)), ((), ())),
                    preferred_element_type=jnp.float32,
                )
                for s in range(per_tile):
                    gain, bias = gains[s]
                    scores[b, s * kpd : (s + 1) * kpd, offset : offset + span] = (
                        affinity[s * kpd : (s + 1) * kpd] * gain + bias
                    )
                for lane in range(offset, offset + span, LANES):
                    value = lse_sublanes(scores[b, :, lane : lane + LANES])
                    store_lse(zz, rt, lane // LANES, value)
            return carry

        lax.fori_loop(0, rt_dev, one, 0)
        send_block(0, zz)

    def later_rows(b):
        for s in range(per_tile):
            pair_shift[s * kpd : (s + 1) * kpd, :] = col_shift[lax.rem(code_of(b, s), tiles)]
        zz = lax.div(b, rt_dev)
        rt = lax.rem(b, rt_dev)
        for lane in range(0, tile, LANES):
            value = lse_sublanes(scores[b, :, lane : lane + LANES] + pair_shift[...])
            store_lse(zz, rt, lane // LANES, value)

    def ag_copy(it, k):
        o = lax.rem(me + k, n)
        return pltpu.make_async_remote_copy(
            src_ref=rows.at[it, me],
            dst_ref=rows.at[it, me],
            send_sem=ag_send.at[o],
            recv_sem=ag_recv.at[me],
            device_id=device(o),
            device_id_type=MESH,
        )

    def wait_block(it, zz):
        for part in range(nq):
            o = zz * nq + part

            @pl.when(o != me)
            def _(o=o):
                pltpu.make_async_copy(rows.at[it, o], rows.at[it, o], ag_recv.at[o]).wait()

    def share_rows(it, row_own):
        def rs_wait(k):
            o = lax.rem(me + k, n)
            pltpu.make_async_copy(parts.at[it, o], parts.at[it, o], rs_recv.at[o]).wait()

        parts[it, me] = lse[me]
        loop(1, n, rs_wait)
        everything = parts[it]
        high = jnp.max(everything, axis=0)
        total = high + jnp.log2(jnp.sum(jnp.exp2(everything - high[None]), axis=0))
        row_own = jnp.minimum(row_own, -total)
        rows[it, me] = row_own
        sends(1, n, lambda k: ag_copy(it, k).start())
        loop(1, n, lambda k: rs_copy(it, lax.rem(me + k, n)).wait_send())
        return row_own

    def columns(it):
        chunk = min(32, kpd)
        pairs = n_imp * rt_dev * per_tile
        width = LANES
        groups = (pairs + width - 1) // width
        best = [jnp.full((kpd, LANES), LOWEST, jnp.float32) for _ in range(tiles)]
        sums = [jnp.zeros((kpd, LANES), jnp.float32) for _ in range(tiles)]
        for g in range(groups):
            first = g * width
            last = min(pairs, first + width)
            pair_shift[0:kpd, :] = jnp.full((kpd, LANES), LOWEST, jnp.float32)

            def one(at_b, tile_of):
                b = lax.rem(z * rt_dev + at_b, n_imp * rt_dev)
                zz = lax.div(b, rt_dev)
                rt = lax.rem(b, rt_dev)

                @pl.when(rt == 0)
                def _():
                    wait_block(it, zz)

                shift = []
                for lane_block in range(tile // LANES):
                    owner = zz * nq + rt * (nq // rt_dev) + lane_block // rr
                    at = lane_block % rr
                    shift.append(rows[it, owner, at : at + 1, :])
                shift = jnp.concatenate(shift, axis=1)
                for s in range(per_tile):
                    here = lane_index == at_b * per_tile + s - first
                    tile_of = jnp.where(here, code_of(b, s), tile_of)
                    for k in range(0, kpd, chunk):
                        got = scores[b, s * kpd + k : s * kpd + k + chunk, :] + shift
                        high = jnp.max(got, axis=1, keepdims=True)
                        total = jnp.sum(jnp.exp2(got - high), axis=1, keepdims=True)
                        pair_shift[k : k + chunk, :] = jnp.where(
                            here, high + jnp.log2(total), pair_shift[k : k + chunk, :]
                        )
                return tile_of

            tile_of = lax.fori_loop(
                first // per_tile,
                last // per_tile,
                one,
                jnp.full((1, LANES), -1, jnp.int32),
            )
            found = pair_shift[0:kpd, :]
            for t in range(tiles):
                mine = jnp.where(tile_of == t, found, LOWEST)
                high = jnp.max(mine, axis=1, keepdims=True)
                new_best = jnp.maximum(best[t], high)
                fresh = jnp.sum(jnp.exp2(mine - new_best), axis=1, keepdims=True)
                if g == 0:
                    sums[t] = jnp.broadcast_to(fresh, (kpd, LANES))
                else:
                    sums[t] = sums[t] * jnp.exp2(best[t] - new_best) + fresh
                best[t] = new_best
        for t in range(tiles):
            old = col_shift[t] if it > 0 else jnp.zeros((kpd, LANES), jnp.float32)
            new = jnp.minimum(old, cap_shift[t] - (best[t] + jnp.log2(sums[t])))
            col_shift[t] = jnp.where(best[t] > NO_ROWS, new, old)

    first_rows(z)
    dcs = range(1, n_rep)
    dxs = range(1, n_camp)

    def forward_z(k):
        for side in range(2):

            @pl.when(has_block(side, k))
            def _(side=side):
                wait_z(side, k)

                @pl.when(has_next(side))
                def _():
                    z_copy(side, k).start()

                for dx in dxs:
                    x_copy(side, k, dx).start()
                for dc in dcs:
                    c_copy(side, k, 0, dc).start()

    def forward_x(k):
        for side in range(2):

            @pl.when(has_block(side, k))
            def _(side=side):
                for dx in dxs:
                    wait_x(side, k, dx)
                    for dc in dcs:
                        c_copy(side, k, dx, dc).start()

    def finish(k):
        for side in range(2):

            @pl.when(has_block(side, k))
            def _(side=side):
                for dx in range(n_camp):
                    for dc in dcs:
                        wait_c(side, k, dx, dc)
                first_rows(block_at(side, k))

    forward_z(1)

    def pump(k):
        forward_z(k + 1)
        forward_x(k)
        finish(k)

    loop(1, n_imp - 1, pump)
    forward_x(n_imp - 1)
    finish(n_imp - 1)

    row_own = jnp.zeros((rr, LANES), jnp.float32)
    for it in range(ITERS):
        if it > 0:

            def later_block(k):
                zz = lax.rem(z + 1 + k, n_imp)
                loop(0, rt_dev, lambda rt: later_rows(zz * rt_dev + rt))
                send_block(1, zz)

            loop(0, n_imp, later_block)
        row_own = share_rows(it, row_own)
        columns(it)
        loop(1, n, lambda k: ag_copy(it, k).wait_send())

    for t in range(tiles):
        flat = jnp.sum(
            jnp.where(eye, col_shift[t, :, 0:kpd], 0.0), axis=0, keepdims=True
        )
        cols[mine, t : t + 1, :] = flat * UNSCALE

    def out_copy(k):
        o = lax.rem(mine + k, n_col)
        return pltpu.make_async_remote_copy(
            src_ref=cols.at[mine],
            dst_ref=cols.at[mine],
            send_sem=out_send.at[o],
            recv_sem=out_recv.at[mine],
            device_id={"imp": lax.div(o, n_rep), "camp": x, "rep": lax.rem(o, n_rep)},
            device_id_type=MESH,
        )

    def out_wait(k):
        o = lax.rem(mine + k, n_col)
        pltpu.make_async_copy(cols.at[o], cols.at[o], out_recv.at[o]).wait()

    sends(1, n_col, lambda k: out_copy(k).start())
    for part in range(nq):
        row_out[part] = rows[ITERS - 1, z * nq + part] * UNSCALE

    def drain(k):
        for side in range(2):

            @pl.when(has_block(side, k))
            def _(side=side):
                @pl.when(has_next(side))
                def _():
                    z_copy(side, k).wait_send()

                for dx in dxs:
                    x_copy(side, k, dx).wait_send()
                for dx in range(n_camp):
                    for dc in dcs:
                        c_copy(side, k, dx, dc).wait_send()

    for side in range(2):

        @pl.when(has_next(side))
        def _(side=side):
            z_copy(side, 0).wait_send()

    loop(1, n_imp, drain)
    loop(1, n_col, lambda k: list_copy(k).wait_send())
    loop(1, n_col, out_wait)
    for t in range(tiles):
        col_out[t] = cols[:, t, :]
    loop(1, n_col, lambda k: out_copy(k).wait_send())


def shards(n_imp, n_camp, n_rep, imp_embed, camp_embed, capacity, tile_lists, tile_counts):
    rt_dev, slots = tile_lists.shape[-2:]
    tiles = camp_embed.shape[0]
    tile = camp_embed.shape[1] * n_imp
    e = camp_embed.shape[2]
    kpd = tile // (n_imp * n_rep)
    nq = n_camp * n_rep
    n = n_imp * nq
    block = rt_dev * tile
    piece = block // nq
    rr = piece // LANES
    n_col = n_imp * n_rep
    per_tile = n_rep * slots
    cfg = (n_imp, n_camp, n_rep, tiles, tile, rt_dev, slots)
    dma = pltpu.SemaphoreType.DMA
    smem = pl.BlockSpec(memory_space=pltpu.SMEM)
    vmem = pl.BlockSpec(memory_space=pltpu.VMEM)
    row_out, col_out = pl.pallas_call(
        functools.partial(kernel, cfg),
        out_shape=(
            jax.ShapeDtypeStruct((nq, rr, LANES), jnp.float32),
            jax.ShapeDtypeStruct((tiles, n_col, kpd), jnp.float32),
        ),
        in_specs=[smem, smem, vmem, vmem, vmem],
        out_specs=(vmem, vmem),
        scratch_shapes=[
            pltpu.VMEM((n_imp, block, e), jnp.bfloat16),
            pltpu.VMEM((n_imp * rt_dev, per_tile * kpd, tile), jnp.float32),
            pltpu.VMEM((per_tile * kpd, e), jnp.bfloat16),
            pltpu.VMEM((n, rr, LANES), jnp.float32),
            pltpu.VMEM((ITERS, n, rr, LANES), jnp.float32),
            pltpu.VMEM((ITERS, n, rr, LANES), jnp.float32),
            pltpu.VMEM((tiles, kpd, LANES), jnp.float32),
            pltpu.VMEM((tiles, kpd, LANES), jnp.float32),
            pltpu.VMEM((per_tile * kpd, LANES), jnp.float32),
            pltpu.VMEM((n_col, tiles, kpd), jnp.float32),
            pltpu.VMEM((n_col, 1, LANES), jnp.int32),
            pltpu.SMEM((n_col, 1, LANES), jnp.int32),
            dma((n_col,)),
            dma((n_col,)),
            dma,
            dma((2, n_imp)),
            dma((2, n_imp)),
            dma((2, n_imp, n_camp)),
            dma((2, n_imp, n_camp)),
            dma((2, n_imp, n_camp, n_rep)),
            dma((2, n_imp, n_camp, n_rep)),
            dma((n,)),
            dma((n,)),
            dma((n,)),
            dma((n,)),
            dma((n_col,)),
            dma((n_col,)),
        ],
        compiler_params=pltpu.CompilerParams(
            collective_id=0, has_side_effects=True, vmem_limit_bytes=56 * 1024 * 1024
        ),
    )(tile_lists, tile_counts, imp_embed, camp_embed, capacity.reshape(tiles, n_col, kpd))
    return (row_out.reshape(-1), col_out.reshape(-1))


def solution(mesh):
    sizes = (mesh.shape["imp"], mesh.shape["camp"], mesh.shape["rep"])
    in_specs = (
        P(("groups", "imp"), None),
        P(("groups", "camp"), "imp", None),
        P(("groups", "camp")),
        P(("groups", "imp"), "camp", "rep", None, None),
        P(("groups", "imp"), "camp", "rep", None),
    )
    out_specs = (P(("groups", "imp")), P(("groups", "camp")))
    return jax.shard_map(
        functools.partial(shards, *sizes),
        mesh=mesh,
        in_specs=in_specs,
        out_specs=out_specs,
        check_vma=False,
    )
```
